128 devices in a mesh: section: 2 (over z_hi), dp: 8 (over z_lo, x), tensor: 8 (over y, core).
Axes of the slice: x: 4, y: 4, z: 4 (z_hi: 2, z_lo: 2; z = z_hi * 2 + z_lo), core: 2. Of those that a mesh axis runs over, the one named last changes fastest.
Arguments:
- act: bfloat16 [512, 8192], P(('section', 'dp', 'tensor')), may hold values from -6 to 6
- gain: float32 [8192], replicated, may hold values from 0.5 to 1.5
- shift: float32 [8192], replicated, may hold values from -3 to 3
- w_in: bfloat16 [8192, 32768], P(('section', 'tensor'), 'dp'), may hold values from -0.0625 to 0.0625
- w_out: bfloat16 [32768, 8192], P('dp', ('section', 'tensor')), may hold values from -0.03125 to 0.03125
- cotangent: bfloat16 [512, 8192], P(None, ('section', 'tensor')), may hold values from -6 to 6
Outputs:
- grad_in: float32 [8192, 32768], P(('section', 'tensor'), 'dp')
- grad_out: float32 [32768, 8192], P('dp', ('section', 'tensor'))
- grad_act: float32 [512, 8192], P(('section', 'dp', 'tensor'))
The draws below stay inside these ranges and needn't reach their ends.
All inputs are finite; a program needn't handle non-finite values.
Results may differ from the reference program's by a relative error of at most 0.0047.
Values may be sent and summed in bfloat16 or wider, within the bound.
No kernel may reach another device: no remote copies, remote signals or barrier semaphores. Data moves between devices by JAX's collectives and lax.ppermute only.
A program may use at most 128 MiB of HBM per device.

```python
import jax
import jax.numpy as jnp
from jax import lax

D = 8192
FF = 32768
TOKENS = 512


def block_scale(stream_key, shape, cuts, smallest, top_value):
    factor_of, own = 1.0, jax.random.fold_in(stream_key, 6)
    for dim, parts in cuts:
        draws = jnp.exp(jax.random.uniform(jax.random.fold_in(own, dim), (parts,), jnp.float32, smallest / len(cuts), top_value / len(cuts)))
        factor_of = factor_of * jnp.repeat(draws, shape[dim] // parts).reshape([-1 if axis == dim else 1 for axis in range(len(shape))])
    return factor_of


def bell_draw(rng, shape, deviation, reach, pieces=(), held_as=jnp.bfloat16):
    values = deviation * jax.random.normal(rng, shape, jnp.float32)
    if pieces:
        values = values * block_scale(rng, shape, pieces, -0.22, 0.18)
    return jnp.clip(values, -reach, reach).astype(held_as)


def setup_inputs(seed: int = 0) -> dict:
    key_list = jax.random.split(jax.random.key(seed), 7)
    act = bell_draw(key_list[0], (TOKENS, D), 1.0, 6.0, ((0, 128),))
    gain = jnp.clip(1.0 + 0.1 * jax.random.normal(key_list[1], (D,), jnp.float32), 0.5, 1.5)
    shift = bell_draw(key_list[2], (D,), 0.5, 3.0, (), jnp.float32)
    w_in = bell_draw(key_list[3], (D, FF), D ** -0.5, 0.0625, ((0, 16), (1, 8)))
    w_out = bell_draw(key_list[4], (FF, D), FF ** -0.5, 0.03125, ((0, 8), (1, 16)))
    cotangent = bell_draw(key_list[5], (TOKENS, D), 1.0, 6.0, ((1, 16),))
    return dict(act=act, gain=gain, shift=shift, w_in=w_in, w_out=w_out, cotangent=cotangent)


EPSILON = 1e-05

def gelu_tanh(inner):
    return jax.nn.gelu(inner, approximate=True)

def reference(act, gain, shift, w_in, w_out, cotangent):
    values = act.astype(jnp.float32)
    center = values - lax.optimization_barrier(jnp.mean(values, axis=1, keepdims=True))
    inverse = lax.rsqrt(lax.optimization_barrier(jnp.mean(center * center, axis=1, keepdims=True)) + EPSILON)
    scaled = center * inverse
    normed = (scaled * gain + shift).astype(jnp.bfloat16)
    preact = jnp.dot(normed, w_in, preferred_element_type=jnp.float32)
    upstream = jnp.dot(cotangent, w_out.T, preferred_element_type=jnp.float32)
    value, pullback = jax.vjp(gelu_tanh, preact)
    hidden = value.astype(jnp.bfloat16)
    pre_grad = pullback(upstream)[0].astype(jnp.bfloat16)
    grad_out = jnp.dot(hidden.T, cotangent, preferred_element_type=jnp.float32)
    grad_in = jnp.dot(normed.T, pre_grad, preferred_element_type=jnp.float32)
    returned = jnp.dot(pre_grad, w_in.T, preferred_element_type=jnp.float32)
    dxhat = returned * gain
    first = lax.optimization_barrier(jnp.mean(dxhat, axis=1, keepdims=True))
    second = lax.optimization_barrier(jnp.mean(dxhat * scaled, axis=1, keepdims=True))
    grad_act = inverse * (dxhat - first - scaled * second)
    return (grad_in, grad_out, grad_act)
```

```python
import jax
import jax.numpy as jnp
from jax import lax
from jax.sharding import PartitionSpec as P

EPSILON = 1e-05
OWNERS = ("section", "tensor")
EVERY = ("section", "dp", "tensor")
BF16, F16, F32 = jnp.bfloat16, jnp.float16, jnp.float32
LIFT = 16.0

LINKS = {
    "core": lambda s, y, c: (s, y, 1 - c),
    "a": lambda s, y, c: (s, y ^ 1, c),
    "b": lambda s, y, c: (s, 3 - y, c),
    "z": lambda s, y, c: (1 - s, y, c),
}


def swap(x, link):
    pairs = []
    for s in range(2):
        for y in range(4):
            for c in range(2):
                s2, y2, c2 = LINKS[link](s, y, c)
                pairs.append((s * 8 + y * 2 + c, s2 * 8 + y2 * 2 + c2))
    return lax.ppermute(x, OWNERS, pairs)


def flip(blocks, number):
    parts = [
        lax.dynamic_index_in_dim(blocks, jnp.bitwise_xor(number, j), 0, keepdims=True)
        for j in range(blocks.shape[0])
    ]
    return jnp.concatenate(parts, axis=0)


ORDERS = (("a", "b", "z"), ("b", "z", "a"), ("z", "a", "b"))


def pick(x, axis, half):
    return lax.index_in_dim(x, half, axis, keepdims=False)


def reduce_blocks(x, order):
    columns = x.shape[1]
    x = x.reshape(2, 2, 2, 64, columns)
    left = ["a", "b", "z"]
    for step, link in enumerate(order):
        axis = left.index(link)
        left.remove(link)
        came = swap(pick(x, axis, 1), link)
        x = pick(x, axis, 0).astype(F32) + came.astype(F32)
        if step < 2:
            x = x.astype(F16)
    return x


def gather_blocks(x, order):
    held = []
    for link in order:
        came = swap(x, link)
        axis = sum(1 for h in held if h < link)
        held.append(link)
        x = jnp.stack([x, came], axis=axis)
    return x.reshape(512, x.shape[-1])


def gelu_tanh(inner):
    return jax.nn.gelu(inner, approximate=True)


def activate(preact, upstream):
    value, pullback = jax.vjp(gelu_tanh, preact)
    return value.astype(BF16), pullback(upstream)[0].astype(BF16)


def matmul(x, y, contract):
    return lax.dot_general(x, y, (contract, ((), ())), preferred_element_type=F32)


def local(act, gain, shift, w_in, w_out, cotangent):
    section, tensor = lax.axis_index("section"), lax.axis_index("tensor")
    core, ring = tensor % 2, tensor // 2
    bit_a = jnp.where((ring == 1) | (ring == 2), 1, 0)
    bit_b = ring // 2
    number = bit_a * 4 + bit_b * 2 + section
    width = w_in.shape[0]
    half = w_in.shape[1] // 2

    out_mine = lax.dynamic_slice_in_dim(w_out, core * half, half, 0)
    out_other = swap(lax.dynamic_slice_in_dim(w_out, (1 - core) * half, half, 0), "core")
    cot = cotangent.reshape(2, 2, 16, 2, 4, width).transpose(3, 0, 1, 2, 4, 5).reshape(8, 64, width)
    cot = flip(cot, number).reshape(512, width)
    cot_other = swap(cot, "core")

    values = act.astype(F32)
    center = values - jnp.mean(values, axis=1, keepdims=True)
    inverse = lax.rsqrt(jnp.mean(center * center, axis=1, keepdims=True) + EPSILON)
    scaled = center * inverse
    normed = (scaled * gain + shift).astype(BF16)

    groups = [[s * 64 + d * 8 + y * 2 + c for s in range(2) for d in range(8) for y in range(4)] for c in range(2)]
    outgoing = normed.reshape(4, 8, 8, 128).transpose(1, 0, 2, 3).reshape(2, 1, 4, 32, 128)
    outgoing = jnp.broadcast_to(outgoing, (2, 8, 4, 32, 128)).reshape(64, 32, 128)
    mixed = lax.all_to_all(outgoing, EVERY, 0, 0, axis_index_groups=groups, tiled=True)
    mine = mixed.reshape(64, 4, 1024).reshape(256, 1024)
    other = swap(mine, "core")
    tokens = jnp.concatenate([mine, other], axis=0).reshape(8, 64, 1024)
    shuffle = jnp.bitwise_xor(number, core * 4)
    tokens = flip(tokens, shuffle).reshape(512, 2, width)
    tok_mine = lax.dynamic_index_in_dim(tokens, core, 1, keepdims=False)
    tok_other = lax.dynamic_index_in_dim(tokens, 1 - core, 1, keepdims=False)

    in_mine = lax.dynamic_slice_in_dim(w_in, core * half, half, 1)
    in_other = swap(lax.dynamic_slice_in_dim(w_in, (1 - core) * half, half, 1), "core")

    cuts = (0, 768, 1408, 2048)
    hidden, pre_grad = [], []
    ups, pres = [], []
    for p, order in enumerate(ORDERS):
        rows = slice(cuts[p], cuts[p + 1])
        up = matmul(cot, out_mine[rows], ((1,), (1,))) + matmul(cot_other, out_other[rows], ((1,), (1,)))
        ups.append(reduce_blocks((up * LIFT).astype(F16), order))
    for p, order in enumerate(ORDERS):
        rows = slice(cuts[p], cuts[p + 1])
        pre = matmul(tok_mine, in_mine[:, rows], ((1,), (0,))) + matmul(tok_other, in_other[:, rows], ((1,), (0,)))
        pres.append(reduce_blocks((pre * LIFT).astype(F16), order))
    for p, order in enumerate(ORDERS):
        h, g = activate(pres[p] * (1.0 / LIFT), ups[p] * (1.0 / LIFT))
        hidden.append(h)
        pre_grad.append(g)
    pre_grad = jnp.concatenate([gather_blocks(g, o) for g, o in zip(pre_grad, ORDERS)], axis=1)
    hidden = jnp.concatenate([gather_blocks(h, o) for h, o in zip(hidden, ORDERS)], axis=1)

    def both(x):
        came = swap(x, "core")
        full = jnp.stack([x, came], axis=0)
        return jnp.concatenate(
            [lax.dynamic_index_in_dim(full, core, 0, keepdims=False), lax.dynamic_index_in_dim(full, 1 - core, 0, keepdims=False)],
            axis=1,
        )

    pre_grad = both(pre_grad)
    share = matmul(pre_grad, w_in, ((1,), (1,))).astype(BF16)
    share = flip(share.reshape(8, 64, width), number)
    share = share.reshape(2, 2, 2, 16, 4, width).transpose(1, 2, 3, 0, 4, 5).reshape(128, 16, 128)
    returned = lax.all_to_all(share, EVERY, 0, 0, tiled=True)
    returned = returned.astype(F32).reshape(2, 8, 8, 4, width).sum(axis=1)
    returned = returned.reshape(16, 4, width).transpose(1, 0, 2).reshape(4, 16 * width)

    hidden = both(hidden)
    grad_in = matmul(tok_mine, pre_grad, ((0,), (0,)))
    grad_out = matmul(hidden, cot, ((0,), (0,)))

    dxhat = returned * gain
    first = jnp.mean(dxhat, axis=1, keepdims=True)
    second = jnp.mean(dxhat * scaled, axis=1, keepdims=True)
    grad_act = inverse * (dxhat - first - scaled * second)
    return (grad_in, grad_out, grad_act)


def solution(mesh):
    in_specs = (
        P(EVERY, None),
        P(),
        P(),
        P(OWNERS, "dp"),
        P("dp", OWNERS),
        P(None, OWNERS),
    )
    out_specs = (P(OWNERS, "dp"), P("dp", OWNERS), P(EVERY, None))
    return jax.shard_map(local, mesh=mesh, in_specs=in_specs, out_specs=out_specs, check_vma=False)
```

```python
import functools

import jax
import jax.numpy as jnp
from jax import lax
from jax.experimental import pallas as pl
from jax.experimental.pallas import tpu as pltpu
from jax.sharding import PartitionSpec as P

EPSILON = 1e-05
OWNERS = ("section", "tensor")
EVERY = ("section", "dp", "tensor")
BF16, F16, F32 = jnp.bfloat16, jnp.float16, jnp.float32
MIB = 1 << 20
LIFT = 16.0

LINKS = {
    "core": lambda s, y, c: (s, y, 1 - c),
    "a": lambda s, y, c: (s, y ^ 1, c),
    "b": lambda s, y, c: (s, 3 - y, c),
    "z": lambda s, y, c: (1 - s, y, c),
}
WEIGHT = {"a": 4, "b": 2, "z": 1}
ORDERS = (("a", "b", "z"), ("b", "z", "a"), ("z", "a", "b"))
TILE = 256
CUTS = (0, 3, 6, 8)


def swap(x, link):
    pairs = []
    for s in range(2):
        for y in range(4):
            for c in range(2):
                s2, y2, c2 = LINKS[link](s, y, c)
                pairs.append((s * 8 + y * 2 + c, s2 * 8 + y2 * 2 + c2))
    return lax.ppermute(x, OWNERS, pairs)


def places(order):
    w = [WEIGHT[link] for link in order]
    return [(q >> 2 & 1) * w[0] + (q >> 1 & 1) * w[1] + (q & 1) * w[2] for q in range(8)]


def lower(shape):
    return lax.broadcasted_iota(jnp.int32, shape, len(shape) - 2) % 8 < 4


def norm_kernel(act, gain, shift, out, twice):
    x = act[...].astype(F32)
    twice[0:4, :] = x
    twice[4:8, :] = x
    x = twice[...]
    center = x - jnp.mean(x, axis=1, keepdims=True)
    inverse = lax.rsqrt(jnp.mean(center * center, axis=1, keepdims=True) + EPSILON)
    twice[...] = center * inverse * gain[...] + shift[...]
    low = lower((8, 128))
    for g in range(16):
        cols = [twice[:, g * 512 + k * 128 : g * 512 + (k + 1) * 128] for k in range(4)]
        piece = jnp.concatenate([jnp.where(low, cols[0], cols[1]), jnp.where(low, cols[2], cols[3])], axis=0)
        piece = piece.astype(BF16)
        for d in range(8):
            out[g // 8, d, g % 8] = piece


def norm_messages(act, gain, shift):
    return pl.pallas_call(
        norm_kernel,
        out_shape=jax.ShapeDtypeStruct((2, 8, 8, 16, 128), BF16),
        scratch_shapes=[pltpu.VMEM((8, 8192), F32)],
        name="norm_messages",
    )(act, gain.reshape(1, -1), shift.reshape(1, -1))


def rows_kernel(x, out):
    even = x[:, 0].astype(F32)
    odd = x[:, 1].astype(F32)
    low = lower((64, 8, 128))
    for k in range(4):
        tile = slice(k // 2 * 8, k // 2 * 8 + 8)
        e, o = even[:, tile], odd[:, tile]
        if k % 2 == 0:
            col = jnp.where(low, e, pltpu.roll(o, 4, 1))
        else:
            col = jnp.where(low, pltpu.roll(e, 4, 1), o)
        out[:, k * 128 : (k + 1) * 128] = col.reshape(512, 128).astype(BF16)


def to_rows(x):
    return pl.pallas_call(
        rows_kernel, out_shape=jax.ShapeDtypeStruct((512, 512), BF16), name="token_rows"
    )(x.reshape(64, 2, 16, 128))


def part_kernel(rel, contract, at, x, x_other, w, w_other, keep, send, lhs):
    @pl.when(pl.program_id(0) == 0)
    def _():
        for q in range(8):
            src = pl.multiple_of(jnp.bitwise_xor(at[0], rel[q]) * 64, 64)
            lhs[0, q * 64 : (q + 1) * 64, :] = x[pl.ds(src, 64), :]
            lhs[1, q * 64 : (q + 1) * 64, :] = x_other[pl.ds(src, 64), :]

    dims = (((1,), (contract,)), ((), ()))
    total = lax.dot_general(lhs[0], w[...], dims, preferred_element_type=F32)
    total = (total + lax.dot_general(lhs[1], w_other[...], dims, preferred_element_type=F32)) * LIFT
    keep[...] = total[:256]
    send[...] = total[256:]


def part_sum(at, x, x_other, w, w_other, part, contract):
    first, tiles = CUTS[part], CUTS[part + 1] - CUTS[part]
    whole = pl.BlockSpec((512, 512), lambda i, at: (0, 0))
    if contract == 1:
        weight = pl.BlockSpec((TILE, 512), lambda i, at: (at[1] * 8 + first + i, 0))
    else:
        weight = pl.BlockSpec((512, TILE), lambda i, at: (0, at[1] * 8 + first + i))
    out = pl.BlockSpec((256, TILE), lambda i, at: (0, i))
    return pl.pallas_call(
        functools.partial(part_kernel, places(ORDERS[part]), contract),
        grid_spec=pltpu.PrefetchScalarGridSpec(
            num_scalar_prefetch=1,
            grid=(tiles,),
            in_specs=[whole, whole, weight, weight],
            out_specs=[out, out],
            scratch_shapes=[pltpu.VMEM((2, 512, 512), BF16)],
        ),
        out_shape=[jax.ShapeDtypeStruct((256, tiles * TILE), F32)] * 2,
        compiler_params=pltpu.CompilerParams(vmem_limit_bytes=16 * MIB),
        cost_estimate=pl.CostEstimate(flops=2 * 512 * 1024 * tiles * TILE, bytes_accessed=4 * MIB, transcendentals=0),
        name="up_part" if contract else "pre_part",
    )(at, x, x_other, w, w_other)


def reduce_blocks(keep, send, order):
    send = send.astype(F16)
    for step, link in enumerate(order):
        came = swap(send, link).astype(F32)
        total = keep + came
        if step == 2:
            return total
        rows = total.shape[0] // 2
        keep, send = total[:rows], total[rows:].astype(F16)


def gather_blocks(x, order):
    x = jnp.concatenate([x, swap(x, order[0])], axis=0)
    x = jnp.concatenate([x, swap(x, order[1])], axis=0)
    return x, swap(x, order[2])


def assemble(at, pieces, whole):
    for h in range(2):
        base = at[1] * 2048 if h == 0 else (1 - at[1]) * 2048
        for p in range(3):
            rel = places(ORDERS[p][::-1])
            first, last = CUTS[p] * TILE, CUTS[p + 1] * TILE
            cols = pl.ds(pl.multiple_of(base + first, TILE), last - first)
            for q in range(8):
                dst = pl.multiple_of(jnp.bitwise_xor(at[0], rel[q]) * 64, 64)
                src = pieces[h * 6 + p * 2 + q // 4]
                whole[pl.ds(dst, 64), cols] = src[q % 4 * 64 : (q % 4 + 1) * 64, :]


def back_kernel(at, *refs):
    pieces, w, whole, out = refs[:12], refs[12], refs[13], refs[14]
    assemble(at, pieces, whole)
    total = jnp.zeros((512, 512), F32)
    for k in range(8):
        cols = slice(k * 512, (k + 1) * 512)
        total += lax.dot_general(whole[:, cols], w[:, cols], (((1,), (1,)), ((), ())), preferred_element_type=F32)
    low = lower((64, 8, 128))
    c = [total[:, k * 128 : (k + 1) * 128].reshape(64, 8, 128) for k in range(4)]
    r = [pltpu.roll(v, 4, 1) for v in c]
    for t in range(2):
        tile = slice(t * 8, t * 8 + 8)
        out[:, 0, tile] = jnp.where(low, c[2 * t], r[2 * t + 1]).astype(BF16)
        out[:, 1, tile] = jnp.where(low, r[2 * t], c[2 * t + 1]).astype(BF16)


SCALARS = pl.BlockSpec(memory_space=pltpu.SMEM)


def back_messages(at, pieces, w_in):
    return pl.pallas_call(
        back_kernel,
        in_specs=[SCALARS] + [pl.BlockSpec(memory_space=pltpu.VMEM)] * 13,
        out_shape=[jax.ShapeDtypeStruct((512, 4096), BF16), jax.ShapeDtypeStruct((64, 2, 16, 128), BF16)],
        compiler_params=pltpu.CompilerParams(vmem_limit_bytes=24 * MIB),
        cost_estimate=pl.CostEstimate(flops=2 * 512 * 512 * 4096, bytes_accessed=12 * MIB, transcendentals=0),
        name="back_messages",
    )(at, *pieces, w_in)


def grad_in_kernel(x, g, out):
    out[...] = jnp.dot(x[...], g[...], preferred_element_type=F32)


def grad_in_of(x_t, g):
    return pl.pallas_call(
        grad_in_kernel,
        grid=(8,),
        in_specs=[pl.BlockSpec((512, 512), lambda i: (0, 0)), pl.BlockSpec((512, 512), lambda i: (0, i))],
        out_specs=pl.BlockSpec((512, 512), lambda i: (0, i)),
        out_shape=jax.ShapeDtypeStruct((512, 4096), F32),
        compiler_params=pltpu.CompilerParams(vmem_limit_bytes=12 * MIB),
        cost_estimate=pl.CostEstimate(flops=2 * 512 * 512 * 4096, bytes_accessed=12 * MIB, transcendentals=0),
        name="grad_in",
    )(x_t, g)


def grad_out_kernel(at, *refs):
    pieces, cot, out, whole = refs[:12], refs[12], refs[13], refs[14]

    @pl.when(pl.program_id(0) == 0)
    def _():
        assemble(at, pieces, whole)

    cols = pl.ds(pl.multiple_of(pl.program_id(0) * 512, 512), 512)
    out[...] = lax.dot_general(whole[:, cols], cot[...], (((0,), (0,)), ((), ())), preferred_element_type=F32)


def grad_out_of(at, pieces, cot):
    return pl.pallas_call(
        grad_out_kernel,
        grid=(8,),
        in_specs=[SCALARS] + [pl.BlockSpec(p.shape, lambda i: (0, 0)) for p in pieces] + [pl.BlockSpec((512, 512), lambda i: (0, 0))],
        out_specs=pl.BlockSpec((512, 512), lambda i: (i, 0)),
        out_shape=jax.ShapeDtypeStruct((4096, 512), F32),
        scratch_shapes=[pltpu.VMEM((512, 4096), BF16)],
        compiler_params=pltpu.CompilerParams(vmem_limit_bytes=24 * MIB),
        cost_estimate=pl.CostEstimate(flops=2 * 512 * 512 * 4096, bytes_accessed=12 * MIB, transcendentals=0),
        name="grad_out",
    )(at, *pieces, cot)


def act_kernel(x, act, gain, out, twice, back):
    a = act[...].astype(F32)
    twice[0:4, :] = a
    twice[4:8, :] = a
    a = twice[...]
    center = a - jnp.mean(a, axis=1, keepdims=True)
    inverse = lax.rsqrt(jnp.mean(center * center, axis=1, keepdims=True) + EPSILON)
    scaled = center * inverse
    low = lower((8, 128))
    for g in range(16):
        total = x[g // 8, 0, g % 8].astype(F32)
        for d in range(1, 8):
            total += x[g // 8, d, g % 8].astype(F32)
        for t in range(2):
            tile = total[t * 8 : t * 8 + 8]
            turned = pltpu.roll(tile, 4, 0)
            at = g * 512 + t * 256
            back[:, at : at + 128] = jnp.where(low, tile, turned)
            back[:, at + 128 : at + 256] = jnp.where(low, turned, tile)
    dxhat = back[...] * gain[...]
    first = jnp.mean(dxhat, axis=1, keepdims=True)
    second = jnp.mean(dxhat * scaled, axis=1, keepdims=True)
    back[...] = inverse * (dxhat - first - scaled * second)
    out[...] = back[0:4, :]


def grad_act_of(x, act, gain):
    return pl.pallas_call(
        act_kernel,
        out_shape=jax.ShapeDtypeStruct((4, 8192), F32),
        scratch_shapes=[pltpu.VMEM((8, 8192), F32), pltpu.VMEM((8, 8192), F32)],
        name="grad_act",
    )(x.reshape(2, 8, 8, 16, 128), act, gain.reshape(1, -1))


def gelu_tanh(inner):
    return jax.nn.gelu(inner, approximate=True)


def activate(preact, upstream):
    value, pullback = jax.vjp(gelu_tanh, preact)
    return value.astype(BF16), pullback(upstream)[0].astype(BF16)


def local(act, gain, shift, w_in, w_out, cotangent):
    section, tensor = lax.axis_index("section"), lax.axis_index("tensor")
    core, ring = tensor % 2, tensor // 2
    bit_a = jnp.where((ring == 1) | (ring == 2), 1, 0)
    number = bit_a * 4 + ring // 2 * 2 + section
    at = jnp.stack([number, core]).astype(jnp.int32)

    out_other = swap(w_out, "core")
    cot_other = swap(cotangent, "core")
    in_other = swap(w_in, "core")

    mixed = lax.all_to_all(norm_messages(act, gain, shift).reshape(128, 16, 128), EVERY, 0, 0, tiled=True)
    mixed_other = swap(mixed, "core")

    ups = []
    for p, order in enumerate(ORDERS):
        ups.append(reduce_blocks(*part_sum(at, cotangent, cot_other, w_out, out_other, p, 1), order))

    tokens = to_rows(mixed)
    tokens_other = to_rows(mixed_other)
    pres = []
    for p, order in enumerate(ORDERS):
        pres.append(reduce_blocks(*part_sum(at, tokens, tokens_other, w_in, in_other, p, 0), order))

    hidden, pre_grad = [], []
    for p in range(3):
        h, g = activate(pres[p] * (1.0 / LIFT), ups[p] * (1.0 / LIFT))
        hidden.append(h)
        pre_grad.append(g)

    def both(parts):
        pieces = [half for x, order in zip(parts, ORDERS) for half in gather_blocks(x, order)]
        return pieces + [swap(piece, "core") for piece in pieces]

    pre_whole, share = back_messages(at, both(pre_grad), w_in)
    returned = lax.all_to_all(share.reshape(128, 16, 128), EVERY, 0, 0, tiled=True)
    grad_act = grad_act_of(returned, act, gain)
    grad_in = grad_in_of(tokens.T, pre_whole)
    grad_out = grad_out_of(at, both(hidden), cotangent)
    return (grad_in, grad_out, grad_act)


def solution(mesh):
    in_specs = (
        P(EVERY, None),
        P(),
        P(),
        P(OWNERS, "dp"),
        P("dp", OWNERS),
        P(None, OWNERS),
    )
    out_specs = (P(OWNERS, "dp"), P("dp", OWNERS), P(EVERY, None))
    return jax.shard_map(local, mesh=mesh, in_specs=in_specs, out_specs=out_specs, check_vma=False)
```

```python
import functools

import jax
import jax.numpy as jnp
from jax import lax
from jax.experimental import pallas as pl
from jax.experimental.pallas import tpu as pltpu
from jax.sharding import PartitionSpec as P

EPSILON = 1e-05
OWNERS = ("section", "tensor")
EVERY = ("section", "dp", "tensor")
BF16, F16, F32 = jnp.bfloat16, jnp.float16, jnp.float32
MIB = 1 << 20
LIFT = 16.0


def swap(x, link):
    pairs = []
    for s in range(2):
        for y in range(4):
            for c in range(2):
                if link == "core":
                    s2, y2, c2 = s, y, 1 - c
                else:
                    y2 = y ^ 1 if link & 4 else y
                    y2 = 3 - y2 if link & 2 else y2
                    s2, c2 = s ^ (link & 1), c
                pairs.append((s * 8 + y * 2 + c, s2 * 8 + y2 * 2 + c2))
    return lax.ppermute(x, OWNERS, pairs)


def lower(shape):
    return lax.broadcasted_iota(jnp.int32, shape, len(shape) - 2) % 8 < 4


SCALARS = pl.BlockSpec(memory_space=pltpu.SMEM)


def norm_kernel(act, gain, shift, out, twice):
    x = act[...].astype(F32)
    twice[0:4, :] = x
    twice[4:8, :] = x
    x = twice[...]
    center = x - jnp.mean(x, axis=1, keepdims=True)
    inverse = lax.rsqrt(jnp.mean(center * center, axis=1, keepdims=True) + EPSILON)
    twice[...] = center * inverse * gain[...] + shift[...]
    low = lower((8, 128))
    for g in range(16):
        cols = [twice[:, g * 512 + k * 128 : g * 512 + (k + 1) * 128] for k in range(4)]
        piece = jnp.concatenate([jnp.where(low, cols[0], cols[1]), jnp.where(low, cols[2], cols[3])], axis=0)
        piece = piece.astype(BF16)
        for d in range(8):
            out[g // 8, d, g % 8] = piece


def norm_messages(act, gain, shift):
    return pl.pallas_call(
        norm_kernel,
        out_shape=pltpu.HBM((2, 8, 8, 16, 128), BF16),
        scratch_shapes=[pltpu.VMEM((8, 8192), F32)],
        name="norm_messages",
    )(act, gain.reshape(1, -1), shift.reshape(1, -1))


def unfold(even, odd, k, low):
    tile = slice(k // 2 * 8, k // 2 * 8 + 8)
    e, o = even[:, tile], odd[:, tile]
    if k % 2 == 0:
        return jnp.where(low, e, pltpu.roll(o, 4, 1))
    return jnp.where(low, pltpu.roll(e, 4, 1), o)


def rows_kernel(x, out):
    even, odd = x[:, 0].astype(F32), x[:, 1].astype(F32)
    low = lower((64, 8, 128))
    for k in range(4):
        out[:, k * 128 : (k + 1) * 128] = unfold(even, odd, k, low).reshape(512, 128).astype(BF16)


ORDERS = ((4, 2, 1), (2, 1, 4), (1, 4, 2))
CUTS = (0, 768, 1536, 2048)


def places(order):
    return [sum(link for k, link in enumerate(order) if q >> (2 - k) & 1) for q in range(8)]


def multiply(step, contract, lhs, w, w_other, outs):
    dims = (((1,), (contract,)), ((), ()))
    total = lax.dot_general(lhs[0], w[...], dims, preferred_element_type=F32)
    total = (total + lax.dot_general(lhs[1], w_other[...], dims, preferred_element_type=F32)) * LIFT
    for p, order in enumerate(ORDERS):
        first, last = max(CUTS[p], step * 1024), min(CUTS[p + 1], step * 1024 + 1024)
        if first >= last:
            continue
        cols = slice(first - CUTS[p], last - CUTS[p])
        for q, j in enumerate(places(order)):
            block = total[j * 64 : (j + 1) * 64, first - step * 1024 : last - step * 1024]
            outs[p * 2 + q // 4][q % 4 * 64 : (q % 4 + 1) * 64, cols] = block


def up_kernel(at, x, x_other, w, w_other, *refs):
    outs, lhs = refs[-7:-1], refs[-1]

    @pl.when(pl.program_id(0) == 0)
    def _():
        for j in range(8):
            src = pl.multiple_of(jnp.bitwise_xor(at[0], j) * 64, 64)
            lhs[0, j * 64 : (j + 1) * 64, :] = x[pl.ds(src, 64), :]
            lhs[1, j * 64 : (j + 1) * 64, :] = x_other[pl.ds(src, 64), :]

    for step in range(2):
        pl.when(pl.program_id(0) == step)(functools.partial(multiply, step, 1, lhs, w, w_other, outs))


def pre_kernel(at, x, x_other, w, w_other, *refs):
    outs, lhs = refs[-7:-1], refs[-1]

    @pl.when(pl.program_id(0) == 0)
    def _():
        low = lower((8, 8, 128))
        for j in range(8):
            src = jnp.bitwise_xor(at[0], j) * 8
            for n, ref in enumerate((x, x_other)):
                even, odd = ref[pl.ds(src, 8), 0].astype(F32), ref[pl.ds(src, 8), 1].astype(F32)
                for k in range(4):
                    rows = unfold(even, odd, k, low).reshape(64, 128).astype(BF16)
                    lhs[n, j * 64 : (j + 1) * 64, k * 128 : (k + 1) * 128] = rows

    for step in range(2):
        pl.when(pl.program_id(0) == step)(functools.partial(multiply, step, 0, lhs, w, w_other, outs))


def chip_sum(at, x, x_other, w, w_other, after, up):
    shape = x.shape
    whole = pl.BlockSpec(shape, lambda i, at: (0,) * len(shape))
    if up:
        weight = pl.BlockSpec((1024, 512), lambda i, at: (at[1] * 2 + i, 0))
    else:
        weight = pl.BlockSpec((512, 1024), lambda i, at: (0, at[1] * 2 + i))
    shapes = [(256, CUTS[p + 1] - CUTS[p]) for p in range(3) for _ in range(2)]
    w, w_other = [pltpu.with_memory_space_constraint(v, pltpu.HBM) for v in (w, w_other)]
    outs = pl.pallas_call(
        up_kernel if up else pre_kernel,
        grid_spec=pltpu.PrefetchScalarGridSpec(
            num_scalar_prefetch=1,
            grid=(2,),
            in_specs=[whole, whole, weight, weight] + [pl.BlockSpec(memory_space=pl.ANY)] * len(after),
            out_specs=[pl.BlockSpec(shape, lambda i, at: (0, 0)) for shape in shapes],
            scratch_shapes=[pltpu.VMEM((2, 512, 512), BF16)],
        ),
        out_shape=[jax.ShapeDtypeStruct(shape, F32) for shape in shapes],
        compiler_params=pltpu.CompilerParams(vmem_limit_bytes=20 * MIB),
        cost_estimate=pl.CostEstimate(flops=2 * 512 * 1024 * 2048, bytes_accessed=9 * MIB, transcendentals=0),
        name="up_sum" if up else "pre_sum",
    )(at, x, x_other, w, w_other, *after)
    return [(outs[2 * p], outs[2 * p + 1].astype(F16)) for p in range(3)]


def halve(keep, send, link):
    total = keep + swap(send, link).astype(F32)
    rows = total.shape[0] // 2
    return total[:rows], total[rows:].astype(F16)


def reduce_pairs(up, pre, order):
    keep = jnp.stack([up[0], pre[0]])
    send = jnp.stack([up[1], pre[1]])
    total = keep + swap(send, order[1]).astype(F32)
    return total[:, :64] + swap(total[:, 64:].astype(F16), order[2]).astype(F32)


def gather_pairs(g, h, order):
    x = jnp.stack([g, h])
    x = jnp.stack([x, swap(x, order[0])])
    came = swap(x, order[1])
    return [jnp.concatenate([x[:, n], came[:, n]]).reshape(256, -1) for n in range(2)]


def assemble(at, pieces, whole):
    for h in range(2):
        base = at[1] * 2048 if h == 0 else (1 - at[1]) * 2048
        for p, order in enumerate(ORDERS):
            cols = pl.ds(pl.multiple_of(base + CUTS[p], 256), CUTS[p + 1] - CUTS[p])
            for q, j in enumerate(places(order[::-1])):
                dst = pl.multiple_of(jnp.bitwise_xor(at[0], j) * 64, 64)
                src = pieces[h * 6 + p * 2 + q // 4]
                whole[pl.ds(dst, 64), cols] = src[q % 4 * 64 : (q % 4 + 1) * 64, :]


def back_kernel(at, *refs):
    pieces, w, out, whole = refs[:12], refs[12], refs[16], refs[20]
    assemble(at, pieces, whole)
    total = jnp.zeros((512, 512), F32)
    for k in range(4):
        cols = slice(k * 1024, (k + 1) * 1024)
        total += lax.dot_general(whole[:, cols], w[:, cols], (((1,), (1,)), ((), ())), preferred_element_type=F32)
    low = lower((64, 8, 128))
    c = [total[:, k * 128 : (k + 1) * 128].reshape(64, 8, 128) for k in range(4)]
    r = [pltpu.roll(v, 4, 1) for v in c]
    for t in range(2):
        tile = slice(t * 8, t * 8 + 8)
        out[:, 0, tile] = jnp.where(low, c[2 * t], r[2 * t + 1]).astype(BF16)
        out[:, 1, tile] = jnp.where(low, r[2 * t], c[2 * t + 1]).astype(BF16)


def back_messages(at, pieces, w_in, later):
    anywhere = pl.BlockSpec(memory_space=pl.ANY)
    outs = pl.pallas_call(
        back_kernel,
        in_specs=[SCALARS] + [pl.BlockSpec(memory_space=pltpu.VMEM)] * 13 + [anywhere] * 3,
        out_specs=[pl.BlockSpec(memory_space=pltpu.VMEM)] + [anywhere] * 3,
        out_shape=[pltpu.HBM((64, 2, 16, 128), BF16)] + [jax.ShapeDtypeStruct(x.shape, x.dtype) for x in later],
        scratch_shapes=[pltpu.VMEM((512, 4096), BF16)],
        input_output_aliases={14 + k: 1 + k for k in range(3)},
        compiler_params=pltpu.CompilerParams(vmem_limit_bytes=20 * MIB),
        cost_estimate=pl.CostEstimate(flops=2 * 512 * 512 * 4096, bytes_accessed=8 * MIB, transcendentals=0),
        name="back_messages",
    )(at, *pieces, w_in, *later)
    return outs[0], outs[1:]


def grad_kernel(out_first, at, *refs):
    pieces, x, out, whole, rows = refs[:12], refs[12], refs[13], refs[14], refs[15]

    @pl.when(pl.program_id(0) == 0)
    def _():
        assemble(at, pieces, whole)
        if not out_first:
            rows_kernel(x, rows)

    cols = pl.ds(pl.multiple_of(pl.program_id(0) * 1024, 1024), 1024)
    dims = (((0,), (0,)), ((), ()))
    if out_first:
        out[...] = lax.dot_general(whole[:, cols], x[...], dims, preferred_element_type=F32)
    else:
        out[...] = lax.dot_general(rows[...], whole[:, cols], dims, preferred_element_type=F32)


def grad_of(at, pieces, x, out_first):
    block, shape = ((1024, 512), (4096, 512)) if out_first else ((512, 1024), (512, 4096))
    pieces = [pltpu.with_memory_space_constraint(p, pltpu.HBM) for p in pieces]
    return pl.pallas_call(
        functools.partial(grad_kernel, out_first),
        grid=(4,),
        in_specs=[SCALARS]
        + [pl.BlockSpec(p.shape, lambda i: (0, 0)) for p in pieces]
        + [pl.BlockSpec(x.shape, lambda i: (0,) * len(x.shape))],
        out_specs=pl.BlockSpec(block, lambda i: (i, 0) if out_first else (0, i)),
        out_shape=jax.ShapeDtypeStruct(shape, F32),
        scratch_shapes=[pltpu.VMEM((512, 4096), BF16), pltpu.VMEM((512, 512), BF16)],
        compiler_params=pltpu.CompilerParams(vmem_limit_bytes=22 * MIB),
        cost_estimate=pl.CostEstimate(flops=2 * 512 * 512 * 4096, bytes_accessed=12 * MIB, transcendentals=0),
        name="grad_out" if out_first else "grad_in",
    )(at, *pieces, x)


def act_kernel(x, act, gain, out, twice, back):
    a = act[...].astype(F32)
    twice[0:4, :] = a
    twice[4:8, :] = a
    a = twice[...]
    center = a - jnp.mean(a, axis=1, keepdims=True)
    inverse = lax.rsqrt(jnp.mean(center * center, axis=1, keepdims=True) + EPSILON)
    scaled = center * inverse
    low = lower((8, 128))
    for g in range(16):
        total = x[g // 8, 0, g % 8].astype(F32)
        for d in range(1, 8):
            total += x[g // 8, d, g % 8].astype(F32)
        for t in range(2):
            tile = total[t * 8 : t * 8 + 8]
            turned = pltpu.roll(tile, 4, 0)
            at = g * 512 + t * 256
            back[:, at : at + 128] = jnp.where(low, tile, turned)
            back[:, at + 128 : at + 256] = jnp.where(low, turned, tile)
    dxhat = back[...] * gain[...]
    first = jnp.mean(dxhat, axis=1, keepdims=True)
    second = jnp.mean(dxhat * scaled, axis=1, keepdims=True)
    back[...] = inverse * (dxhat - first - scaled * second)
    out[...] = back[0:4, :]


def grad_act_of(x, act, gain):
    return pl.pallas_call(
        act_kernel,
        out_shape=jax.ShapeDtypeStruct((4, 8192), F32),
        scratch_shapes=[pltpu.VMEM((8, 8192), F32), pltpu.VMEM((8, 8192), F32)],
        name="grad_act",
    )(x.reshape(2, 8, 8, 16, 128), act, gain.reshape(1, -1))


def gelu_tanh(inner):
    return jax.nn.gelu(inner, approximate=True)


def activate(preact, upstream):
    value, pullback = jax.vjp(gelu_tanh, preact)
    return value.astype(BF16), pullback(upstream)[0].astype(BF16)


def local(act, gain, shift, w_in, w_out, cotangent):
    section, tensor = lax.axis_index("section"), lax.axis_index("tensor")
    core, ring = lax.bitwise_and(tensor, 1), lax.shift_right_logical(tensor, 1)
    bit_a = jnp.where((ring == 1) | (ring == 2), 1, 0)
    number = bit_a * 4 + lax.bitwise_and(ring, 2) + section
    at = jnp.stack([number, core]).astype(jnp.int32)

    out_other = swap(w_out, "core")
    cot_other = swap(cotangent, "core")
    in_other = swap(w_in, "core")
    messages = norm_messages(act, gain, shift)
    mixed = lax.all_to_all(messages.reshape(128, 16, 128), EVERY, 0, 0, tiled=True).reshape(64, 2, 16, 128)
    up = chip_sum(at, cotangent, cot_other, w_out, out_other, [], True)
    up = [halve(*pair, order[0]) for pair, order in zip(up, ORDERS)]
    mixed_other = swap(mixed, "core")
    pre = chip_sum(at, mixed, mixed_other, w_in, in_other, [pair[0] for pair in up], False)
    pre = [halve(*pair, order[0]) for pair, order in zip(pre, ORDERS)]
    pre_grad, hidden = [], []
    for u, v, order in zip(up, pre, ORDERS):
        total = reduce_pairs(u, v, order) * (1.0 / LIFT)
        h, g = activate(total[1], total[0])
        g, h = gather_pairs(g, h, order)
        pre_grad += [g, swap(g, order[2])]
        hidden.append(h)

    def both(pieces):
        return pieces + [swap(p, "core") for p in pieces]

    pre_grad = both(pre_grad)
    share, hidden = back_messages(at, pre_grad, w_in, hidden)
    hidden = [p for h, order in zip(hidden, ORDERS) for p in (h, swap(h, order[2]))]
    returned = lax.all_to_all(share.reshape(128, 16, 128), EVERY, 0, 0, tiled=True)
    grad_act = grad_act_of(returned, act, gain)
    grad_in = grad_of(at, pre_grad, mixed, False)
    grad_out = grad_of(at, both(hidden), cotangent, True)
    return (grad_in, grad_out, grad_act)


def solution(mesh):
    in_specs = (
        P(EVERY, None),
        P(),
        P(),
        P(OWNERS, "dp"),
        P("dp", OWNERS),
        P(None, OWNERS),
    )
    out_specs = (P(OWNERS, "dp"), P("dp", OWNERS), P(EVERY, None))
    return jax.shard_map(local, mesh=mesh, in_specs=in_specs, out_specs=out_specs, check_vma=False)
```

```python
import functools

import jax
import jax.numpy as jnp
from jax import lax
from jax.experimental import pallas as pl
from jax.experimental.pallas import tpu as pltpu
from jax.sharding import PartitionSpec as P

EPSILON = 1e-05
OWNERS = ("section", "tensor")
EVERY = ("section", "dp", "tensor")
BF16, F32 = jnp.bfloat16, jnp.float32
MIB = 1 << 20

def swap(x, link):
    pairs = []
    for s in range(2):
        for y in range(4):
            for c in range(2):
                if link == "core":
                    s2, y2, c2 = s, y, 1 - c
                else:
                    y2 = y ^ 1 if link & 4 else y
                    y2 = 3 - y2 if link & 2 else y2
                    s2, c2 = s ^ (link & 1), c
                pairs.append((s * 8 + y * 2 + c, s2 * 8 + y2 * 2 + c2))
    return lax.ppermute(x, OWNERS, pairs)


def lower(shape):
    return lax.broadcasted_iota(jnp.int32, shape, len(shape) - 2) % 8 < 4


SCALARS = pl.BlockSpec(memory_space=pltpu.SMEM)


def norm_kernel(act, gain, shift, out, twice):
    x = act[...].astype(F32)
    twice[0:4, :] = x
    twice[4:8, :] = x
    x = twice[...]
    center = x - jnp.mean(x, axis=1, keepdims=True)
    inverse = lax.rsqrt(jnp.mean(center * center, axis=1, keepdims=True) + EPSILON)
    twice[...] = center * inverse * gain[...] + shift[...]
    low = lower((8, 128))
    for g in range(16):
        cols = [twice[:, g * 512 + k * 128 : g * 512 + (k + 1) * 128] for k in range(4)]
        piece = jnp.concatenate([jnp.where(low, cols[0], cols[1]), jnp.where(low, cols[2], cols[3])], axis=0)
        piece = piece.astype(BF16)
        for d in range(8):
            out[g // 8, d, g % 8] = piece


def norm_messages(act, gain, shift):
    return pl.pallas_call(
        norm_kernel,
        out_shape=pltpu.HBM((2, 8, 8, 16, 128), BF16),
        scratch_shapes=[pltpu.VMEM((8, 8192), F32)],
        name="norm_messages",
    )(act, gain.reshape(1, -1), shift.reshape(1, -1))


def unfold(even, odd, k, low):
    tile = slice(k // 2 * 8, k // 2 * 8 + 8)
    e, o = even[:, tile], odd[:, tile]
    if k % 2 == 0:
        return jnp.where(low, e, pltpu.roll(o, 4, 1))
    return jnp.where(low, pltpu.roll(e, 4, 1), o)


def rows_kernel(x, out):
    even, odd = x[:, 0].astype(F32), x[:, 1].astype(F32)
    low = lower((64, 8, 128))
    for k in range(4):
        out[:, k * 128 : (k + 1) * 128] = unfold(even, odd, k, low).reshape(512, 128).astype(BF16)


ORDERS = ((4, 2, 1), (2, 1, 4), (1, 4, 2))
CUTS = (0, 768, 1536, 2048)


def places(order):
    return [sum(link for k, link in enumerate(order) if q >> (2 - k) & 1) for q in range(8)]


def multiply(step, contract, lhs, w, w_other, outs):
    dims = (((1,), (contract,)), ((), ()))
    total = lax.dot_general(lhs[0], w[...], dims, preferred_element_type=F32)
    total = total + lax.dot_general(lhs[1], w_other[...], dims, preferred_element_type=F32)
    for p, order in enumerate(ORDERS):
        first, last = max(CUTS[p], step * 1024), min(CUTS[p + 1], step * 1024 + 1024)
        if first >= last:
            continue
        cols = slice(first - CUTS[p], last - CUTS[p])
        for q, j in enumerate(places(order)):
            block = total[j * 64 : (j + 1) * 64, first - step * 1024 : last - step * 1024]
            outs[p * 2 + q // 4][q % 4 * 64 : (q % 4 + 1) * 64, cols] = block.astype(outs[p * 2 + q // 4].dtype)


def up_kernel(at, x, x_other, w, w_other, *refs):
    outs, lhs = refs[-7:-1], refs[-1]

    @pl.when(pl.program_id(0) == 0)
    def _():
        for j in range(8):
            src = pl.multiple_of(jnp.bitwise_xor(at[0], j) * 64, 64)
            lhs[0, j * 64 : (j + 1) * 64, :] = x[pl.ds(src, 64), :]
            lhs[1, j * 64 : (j + 1) * 64, :] = x_other[pl.ds(src, 64), :]

    for step in range(2):
        pl.when(pl.program_id(0) == step)(functools.partial(multiply, step, 1, lhs, w, w_other, outs))


def pre_kernel(at, x, x_other, w, w_other, *refs):
    outs, lhs = refs[-7:-1], refs[-1]

    @pl.when(pl.program_id(0) == 0)
    def _():
        low = lower((8, 8, 128))
        for j in range(8):
            src = jnp.bitwise_xor(at[0], j) * 8
            for n, ref in enumerate((x, x_other)):
                even, odd = ref[pl.ds(src, 8), 0].astype(F32), ref[pl.ds(src, 8), 1].astype(F32)
                for k in range(4):
                    rows = unfold(even, odd, k, low).reshape(64, 128).astype(BF16)
                    lhs[n, j * 64 : (j + 1) * 64, k * 128 : (k + 1) * 128] = rows

    for step in range(2):
        pl.when(pl.program_id(0) == step)(functools.partial(multiply, step, 0, lhs, w, w_other, outs))


def chip_sum(at, x, x_other, w, w_other, after, up):
    shape = x.shape
    whole = pl.BlockSpec(shape, lambda i, at: (0,) * len(shape))
    if up:
        weight = pl.BlockSpec((1024, 512), lambda i, at: (at[1] * 2 + i, 0))
    else:
        weight = pl.BlockSpec((512, 1024), lambda i, at: (0, at[1] * 2 + i))
    shapes = [(256, CUTS[p + 1] - CUTS[p]) for p in range(3) for _ in range(2)]
    w, w_other = [pltpu.with_memory_space_constraint(v, pltpu.HBM) for v in (w, w_other)]
    outs = pl.pallas_call(
        up_kernel if up else pre_kernel,
        grid_spec=pltpu.PrefetchScalarGridSpec(
            num_scalar_prefetch=1,
            grid=(2,),
            in_specs=[whole, whole, weight, weight] + [pl.BlockSpec(memory_space=pl.ANY)] * len(after),
            out_specs=[pl.BlockSpec(shape, lambda i, at: (0, 0)) for shape in shapes],
            scratch_shapes=[pltpu.VMEM((2, 512, 512), BF16)],
        ),
        out_shape=[jax.ShapeDtypeStruct(shape, BF16 if k % 2 else F32) for k, shape in enumerate(shapes)],
        compiler_params=pltpu.CompilerParams(vmem_limit_bytes=20 * MIB),
        cost_estimate=pl.CostEstimate(flops=2 * 512 * 1024 * 2048, bytes_accessed=9 * MIB, transcendentals=0),
        name="up_sum" if up else "pre_sum",
    )(at, x, x_other, w, w_other, *after)
    return [(outs[2 * p], outs[2 * p + 1]) for p in range(3)]


def first_kernel(*refs):
    for p in range(3):
        for n in range(2):
            keep, came = refs[p * 4 + n * 2], refs[p * 4 + n * 2 + 1]
            total = keep[...] + came[...].astype(F32)
            refs[12 + p * 2][n] = total[:128]
            refs[13 + p * 2][n] = total[128:].astype(BF16)


def second_kernel(*refs):
    for p in range(3):
        total = refs[p * 2][...] + refs[p * 2 + 1][...].astype(F32)
        refs[6 + p * 2][...] = total
        refs[7 + p * 2][...] = total.astype(BF16)


def third_kernel(*refs):
    for p in range(3):
        keep, came, out = refs[p * 2], refs[p * 2 + 1], refs[6 + p]
        for block in range(2):
            mine, theirs = slice(block * 64, block * 64 + 64), slice(64 - block * 64, 128 - block * 64)
            for first in range(0, out.shape[2], 128):
                cols = slice(first, first + 128)
                up = keep[0, mine, cols] + came[0, theirs, cols].astype(F32)
                v = keep[1, mine, cols] + came[1, theirs, cols].astype(F32)
                square = v * v
                t = jnp.tanh(SLOPE * v * (1.0 + CUBE * square))
                half = 0.5 * (1.0 + t)
                out[1, mine, cols] = (v * half).astype(BF16)
                bend = 0.5 * SLOPE * v * (1.0 - t * t) * (1.0 + 3.0 * CUBE * square)
                out[0, mine, cols] = (up * (half + bend)).astype(BF16)


SLOPE, CUBE = 0.7978845608028654, 0.044715


def joint(kernel, name, arrays, shapes):
    outs = pl.pallas_call(
        kernel,
        in_specs=[pl.BlockSpec(memory_space=pltpu.VMEM)] * len(arrays),
        out_specs=[pl.BlockSpec(memory_space=pltpu.VMEM)] * len(shapes),
        out_shape=[jax.ShapeDtypeStruct(*shape) for shape in shapes],
        compiler_params=pltpu.CompilerParams(vmem_limit_bytes=16 * MIB),
        cost_estimate=pl.CostEstimate(flops=MIB, bytes_accessed=MIB, transcendentals=0),
        name=name,
    )(*arrays)
    return list(outs)


def exchange_sums(up, pre):
    widths = [CUTS[p + 1] - CUTS[p] for p in range(3)]
    arrays = []
    for p, order in enumerate(ORDERS):
        for keep, send in (up[p], pre[p]):
            arrays += [keep, swap(send, order[0])]
    pair = [((2, 128, width), dtype) for width in widths for dtype in (F32, BF16)]
    left = joint(first_kernel, "first_sums", arrays, pair)
    for p, order in enumerate(ORDERS):
        left[p * 2 + 1] = swap(left[p * 2 + 1], order[1])
    left = joint(second_kernel, "second_sums", left, pair)
    for p, order in enumerate(ORDERS):
        left[p * 2 + 1] = swap(left[p * 2 + 1], order[2])
    return joint(third_kernel, "third_sums", left, [((2, 128, width), BF16) for width in widths])


def fourth_kernel(*refs):
    for p in range(3):
        for k in range(2):
            refs[6 + p][k] = refs[p * 2 + k][...]


def gather(parts):
    arrays = []
    for x, order in zip(parts, ORDERS):
        arrays += [x, swap(x, order[1])]
    held = joint(fourth_kernel, "fourth_blocks", arrays, [((2, *x.shape), BF16) for x in parts])
    pieces = []
    for x, order in zip(held, ORDERS):
        pieces += [x, swap(x, order[0])]
    return pieces


def assemble(at, pieces, whole):
    for h in range(2):
        base = at[1] * 2048 if h == 0 else (1 - at[1]) * 2048
        for p, order in enumerate(ORDERS):
            cols = pl.ds(pl.multiple_of(base + CUTS[p], 256), CUTS[p + 1] - CUTS[p])
            for q, j in enumerate(places(order)):
                dst = pl.multiple_of(jnp.bitwise_xor(at[0], j) * 64, 64)
                src = pieces[h * 6 + p * 2 + q // 4]
                whole[pl.ds(dst, 64), cols] = src[q // 2 % 2, 0, q % 2 * 64 : q % 2 * 64 + 64, :]


def back_kernel(at, *refs):
    pieces, w, out, whole = refs[:12], refs[12], refs[13], refs[14]
    assemble(at, pieces, whole)
    total = jnp.zeros((512, 512), F32)
    for k in range(4):
        cols = slice(k * 1024, (k + 1) * 1024)
        total += lax.dot_general(whole[:, cols], w[:, cols], (((1,), (1,)), ((), ())), preferred_element_type=F32)
    low = lower((64, 8, 128))
    c = [total[:, k * 128 : (k + 1) * 128].reshape(64, 8, 128) for k in range(4)]
    r = [pltpu.roll(v, 4, 1) for v in c]
    for t in range(2):
        tile = slice(t * 8, t * 8 + 8)
        out[:, 0, tile] = jnp.where(low, c[2 * t], r[2 * t + 1]).astype(BF16)
        out[:, 1, tile] = jnp.where(low, r[2 * t], c[2 * t + 1]).astype(BF16)


def back_messages(at, pieces, w_in):
    return pl.pallas_call(
        back_kernel,
        in_specs=[SCALARS] + [pl.BlockSpec(memory_space=pltpu.VMEM)] * 13,
        out_specs=pl.BlockSpec(memory_space=pltpu.VMEM),
        out_shape=pltpu.HBM((64, 2, 16, 128), BF16),
        scratch_shapes=[pltpu.VMEM((512, 4096), BF16)],
        compiler_params=pltpu.CompilerParams(vmem_limit_bytes=24 * MIB),
        cost_estimate=pl.CostEstimate(flops=2 * 512 * 512 * 4096, bytes_accessed=8 * MIB, transcendentals=0),
        name="back_messages",
    )(at, *pieces, w_in)


def grads_kernel(at, *refs):
    pieces, (x, cot, grad_in, grad_out), scratch = refs[:12], refs[12:16], refs[16:]
    held, rows, turned, wide_in, wide_out, loads, stores = scratch
    todo = [(p, h) for p in range(3) for h in range(2)]
    arrivals = {}
    for p, h in todo:
        for which in range(2):
            for k in range(2):
                n = h * 6 + p * 2 + k
                target = held.at[which, h * 3 + p, k, :, :, 0 : CUTS[p + 1] - CUTS[p]]
                copy = pltpu.make_async_copy(pieces[n].at[:, which], target, loads.at[which * 12 + n])
                copy.start()
                arrivals[which, h, p, k] = copy
    rows_kernel(x, rows)
    dims = (((0,), (0,)), ((), ()))
    leaving = []

    def send(buffer, target):
        leaving.append(pltpu.make_async_copy(buffer, target, stores.at[len(leaving)]))
        leaving[-1].start()

    for p, h in todo:
        if h == 0:
            for q, j in enumerate(places(ORDERS[p])):
                src = pl.multiple_of(jnp.bitwise_xor(at[0], j) * 64, 64)
                turned[0, q * 64 : (q + 1) * 64, :] = rows[pl.ds(src, 64), :]
                turned[1, q * 64 : (q + 1) * 64, :] = cot[pl.ds(src, 64), :]
        for which in range(2):
            for k in range(2):
                arrivals[which, h, p, k].wait()
            for first in range(0, CUTS[p + 1] - CUTS[p], 256):
                piece = held[which, h * 3 + p, :, :, :, first : first + 256].reshape(512, 256)
                slot = (h * 2048 + CUTS[p] + first) // 256
                base = (at[1] if h == 0 else 1 - at[1]) * 2048 + CUTS[p] + first
                span = pl.ds(pl.multiple_of(base, 256), 256)
                if which == 0:
                    wide_in[slot] = lax.dot_general(turned[0], piece, dims, preferred_element_type=F32)
                    send(wide_in.at[slot], grad_in.at[:, span])
                else:
                    wide_out[slot] = lax.dot_general(piece, turned[1], dims, preferred_element_type=F32)
                    send(wide_out.at[slot], grad_out.at[span, :])
    for copy in leaving:
        copy.wait()


def grads_of(at, pieces, x, cot):
    anywhere, vmem = pl.BlockSpec(memory_space=pl.ANY), pl.BlockSpec(memory_space=pltpu.VMEM)
    pieces = [pltpu.with_memory_space_constraint(p, pltpu.HBM) for p in pieces]
    return pl.pallas_call(
        grads_kernel,
        in_specs=[SCALARS] + [anywhere] * 12 + [vmem] * 2,
        out_specs=[anywhere] * 2,
        out_shape=[pltpu.HBM((512, 4096), F32), pltpu.HBM((4096, 512), F32)],
        scratch_shapes=[
            pltpu.VMEM((2, 6, 2, 2, 128, 768), BF16),
            pltpu.VMEM((512, 512), BF16),
            pltpu.VMEM((2, 512, 512), BF16),
            pltpu.VMEM((16, 512, 256), F32),
            pltpu.VMEM((16, 256, 512), F32),
            pltpu.SemaphoreType.DMA((24,)),
            pltpu.SemaphoreType.DMA((32,)),
        ],
        compiler_params=pltpu.CompilerParams(vmem_limit_bytes=36 * MIB),
        cost_estimate=pl.CostEstimate(flops=4 * 512 * 512 * 4096, bytes_accessed=24 * MIB, transcendentals=0),
        name="grads",
    )(at, *pieces, x, cot)


def act_kernel(x, act, gain, out, twice, back):
    a = act[...].astype(F32)
    twice[0:4, :] = a
    twice[4:8, :] = a
    a = twice[...]
    center = a - jnp.mean(a, axis=1, keepdims=True)
    inverse = lax.rsqrt(jnp.mean(center * center, axis=1, keepdims=True) + EPSILON)
    scaled = center * inverse
    low = lower((8, 128))
    for g in range(16):
        total = x[g // 8, 0, g % 8].astype(F32)
        for d in range(1, 8):
            total += x[g // 8, d, g % 8].astype(F32)
        for t in range(2):
            tile = total[t * 8 : t * 8 + 8]
            turned = pltpu.roll(tile, 4, 0)
            at = g * 512 + t * 256
            back[:, at : at + 128] = jnp.where(low, tile, turned)
            back[:, at + 128 : at + 256] = jnp.where(low, turned, tile)
    dxhat = back[...] * gain[...]
    first = jnp.mean(dxhat, axis=1, keepdims=True)
    second = jnp.mean(dxhat * scaled, axis=1, keepdims=True)
    back[...] = inverse * (dxhat - first - scaled * second)
    out[...] = back[0:4, :]


def grad_act_of(x, act, gain):
    return pl.pallas_call(
        act_kernel,
        out_shape=jax.ShapeDtypeStruct((4, 8192), F32),
        scratch_shapes=[pltpu.VMEM((8, 8192), F32), pltpu.VMEM((8, 8192), F32)],
        name="grad_act",
    )(x.reshape(2, 8, 8, 16, 128), act, gain.reshape(1, -1))


def local(act, gain, shift, w_in, w_out, cotangent):
    section, tensor = lax.axis_index("section"), lax.axis_index("tensor")
    core, ring = lax.bitwise_and(tensor, 1), lax.shift_right_logical(tensor, 1)
    bit_a = jnp.where((ring == 1) | (ring == 2), 1, 0)
    number = bit_a * 4 + lax.bitwise_and(ring, 2) + section
    at = jnp.stack([number, core]).astype(jnp.int32)

    out_other = swap(w_out, "core")
    cot_other = swap(cotangent, "core")
    in_other = swap(w_in, "core")
    messages = norm_messages(act, gain, shift)
    mixed = lax.all_to_all(messages.reshape(128, 16, 128), EVERY, 0, 0, tiled=True).reshape(64, 2, 16, 128)
    mixed_other = swap(mixed, "core")
    up = chip_sum(at, cotangent, cot_other, w_out, out_other, [], True)
    pre = chip_sum(at, mixed, mixed_other, w_in, in_other, [up[0][0]], False)
    pieces = gather(exchange_sums(up, pre))
    pieces += [swap(p, "core") for p in pieces]

    share = back_messages(at, pieces, w_in)
    returned = lax.all_to_all(share.reshape(128, 16, 128), EVERY, 0, 0, tiled=True)
    grad_act = grad_act_of(returned, act, gain)
    grad_in, grad_out = grads_of(at, pieces, mixed, cotangent)
    return (grad_in, grad_out, grad_act)


def solution(mesh):
    in_specs = (
        P(EVERY, None),
        P(),
        P(),
        P(OWNERS, "dp"),
        P("dp", OWNERS),
        P(None, OWNERS),
    )
    out_specs = (P(OWNERS, "dp"), P("dp", OWNERS), P(EVERY, None))
    return jax.shard_map(local, mesh=mesh, in_specs=in_specs, out_specs=out_specs, check_vma=False)
```

```python
import functools

import jax
import jax.numpy as jnp
from jax import lax
from jax.experimental import pallas as pl
from jax.experimental.pallas import tpu as pltpu
from jax.sharding import PartitionSpec as P

EPSILON = 1e-05
OWNERS = ("section", "tensor")
EVERY = ("section", "dp", "tensor")
BF16, F32 = jnp.bfloat16, jnp.float32
MIB = 1 << 20

def swap(x, link):
    pairs = []
    for s in range(2):
        for y in range(4):
            for c in range(2):
                if link == "core":
                    s2, y2, c2 = s, y, 1 - c
                else:
                    y2 = y ^ 1 if link & 4 else y
                    y2 = 3 - y2 if link & 2 else y2
                    s2, c2 = s ^ (link & 1), c
                pairs.append((s * 8 + y * 2 + c, s2 * 8 + y2 * 2 + c2))
    return lax.ppermute(x, OWNERS, pairs)


def lower(shape):
    return lax.broadcasted_iota(jnp.int32, shape, len(shape) - 2) % 8 < 4


SCALARS = pl.BlockSpec(memory_space=pltpu.SMEM)


def norm_kernel(act, gain, shift, out, twice):
    x = act[...].astype(F32)
    twice[0:4, :] = x
    twice[4:8, :] = x
    x = twice[...]
    center = x - jnp.mean(x, axis=1, keepdims=True)
    inverse = lax.rsqrt(jnp.mean(center * center, axis=1, keepdims=True) + EPSILON)
    twice[...] = center * inverse * gain[...] + shift[...]
    low = lower((8, 128))
    for g in range(16):
        cols = [twice[:, g * 512 + k * 128 : g * 512 + (k + 1) * 128] for k in range(4)]
        piece = jnp.concatenate([jnp.where(low, cols[0], cols[1]), jnp.where(low, cols[2], cols[3])], axis=0)
        piece = piece.astype(BF16)
        for d in range(8):
            out[g // 8, d, g % 8] = piece


def norm_messages(act, gain, shift):
    return pl.pallas_call(
        norm_kernel,
        out_shape=pltpu.HBM((2, 8, 8, 16, 128), BF16),
        scratch_shapes=[pltpu.VMEM((8, 8192), F32)],
        compiler_params=pltpu.CompilerParams(vmem_limit_bytes=56 * MIB),
        name="norm_messages",
    )(act, gain.reshape(1, -1), shift.reshape(1, -1))


def unfold(even, odd, k, low):
    tile = slice(k // 2 * 8, k // 2 * 8 + 8)
    e, o = even[:, tile], odd[:, tile]
    if k % 2 == 0:
        return jnp.where(low, e, pltpu.roll(o, 4, 1))
    return jnp.where(low, pltpu.roll(e, 4, 1), o)


def rows_kernel(x, out):
    x = x[...].reshape(64, 2, 16, 128)
    even, odd = x[:, 0].astype(F32), x[:, 1].astype(F32)
    low = lower((64, 8, 128))
    for k in range(4):
        out[:, k * 128 : (k + 1) * 128] = unfold(even, odd, k, low).reshape(512, 128).astype(BF16)


ORDERS = ((4, 2, 1), (2, 1, 4), (1, 4, 2))
CUTS = (0, 768, 1536, 2048)


def places(order):
    return [sum(link for k, link in enumerate(order) if q >> (2 - k) & 1) for q in range(8)]


def split(total, first_column, outs):
    last_column = first_column + total.shape[1]
    for p, order in enumerate(ORDERS):
        first, last = max(CUTS[p], first_column), min(CUTS[p + 1], last_column)
        if first >= last:
            continue
        for q, j in enumerate(places(order)):
            out = outs[p * 2 + q // 4]
            block = total[j * 64 : (j + 1) * 64, first - first_column : last - first_column]
            out[q % 4 * 64 : (q % 4 + 1) * 64, first - CUTS[p] : last - CUTS[p]] = block.astype(out.dtype)


def up_kernel(at, x, x_other, w, w_other, *refs):
    outs, (lhs, weights, loads) = refs[:6], refs[6:]
    span = pl.ds(pl.multiple_of(at[1] * 2048, 2048), 2048)
    copies = []
    for n, ref in enumerate((w, w_other)):
        copies.append(pltpu.make_async_copy(ref.at[span, :], weights.at[:, n * 512 : n * 512 + 512], loads.at[n]))
        copies[n].start()
    for j in range(8):
        src = pl.multiple_of(jnp.bitwise_xor(at[0], j) * 64, 64)
        lhs[j * 64 : (j + 1) * 64, 0:512] = x[pl.ds(src, 64), :]
        lhs[j * 64 : (j + 1) * 64, 512:1024] = x_other[pl.ds(src, 64), :]
    for copy in copies:
        copy.wait()
    for first in (0, 1024):
        dims = (((1,), (1,)), ((), ()))
        split(lax.dot_general(lhs[...], weights[first : first + 1024], dims, preferred_element_type=F32), first, outs)


def pre_kernel(at, x, x_other, w, w_other, *refs):
    outs, (lhs, weights, tokens, loads, token_loads) = refs[:6], refs[6:]
    copies = [pltpu.make_async_copy(ref, tokens.at[n], token_loads.at[n]) for n, ref in enumerate((x, x_other))]
    for k in range(2):
        for n, ref in enumerate((w, w_other)):
            source = ref.at[:, pl.ds(pl.multiple_of(at[1] * 2048 + k * 1024, 1024), 1024)]
            target = weights.at[n * 512 : n * 512 + 512, k * 1024 : k * 1024 + 1024]
            copies.append(pltpu.make_async_copy(source, target, loads.at[k * 2 + n]))
    for copy in copies:
        copy.start()
    low = lower((8, 8, 128))
    for n in range(2):
        copies[n].wait()
        for j in range(8):
            some = tokens[n, pl.ds(jnp.bitwise_xor(at[0], j) * 16, 16)].reshape(8, 2, 16, 128)
            even, odd = some[:, 0].astype(F32), some[:, 1].astype(F32)
            for k in range(4):
                rows = unfold(even, odd, k, low).reshape(64, 128).astype(BF16)
                lhs[j * 64 : (j + 1) * 64, n * 512 + k * 128 : n * 512 + (k + 1) * 128] = rows
    for k in range(2):
        copies[2 + 2 * k].wait()
        copies[3 + 2 * k].wait()
        split(jnp.dot(lhs[...], weights[:, k * 1024 : k * 1024 + 1024], preferred_element_type=F32), k * 1024, outs)


HALVES = [
    jax.ShapeDtypeStruct((256, CUTS[p + 1] - CUTS[p]), dtype) for p in range(3) for dtype in (F32, BF16)
]
VMEM_BLOCK, ANY_BLOCK = pl.BlockSpec(memory_space=pltpu.VMEM), pl.BlockSpec(memory_space=pl.ANY)


def in_pairs(arrays):
    return [(arrays[2 * p], arrays[2 * p + 1]) for p in range(3)]


def chip_sum(at, x, x_other, w, w_other, up):
    w, w_other = [pltpu.with_memory_space_constraint(v, pltpu.HBM) for v in (w, w_other)]
    scratch = [pltpu.VMEM((512, 1024), BF16), pltpu.VMEM((2048, 1024) if up else (1024, 2048), BF16)]
    loads = [pltpu.SemaphoreType.DMA((2,))]
    if not up:
        scratch.append(pltpu.VMEM((2, 128, 16, 128), BF16))
        loads.insert(0, pltpu.SemaphoreType.DMA((4,)))
    outs = pl.pallas_call(
        up_kernel if up else pre_kernel,
        in_specs=[SCALARS] + [VMEM_BLOCK if up else ANY_BLOCK] * 2 + [ANY_BLOCK] * 2,
        out_specs=[VMEM_BLOCK] * 6,
        out_shape=HALVES,
        scratch_shapes=scratch + loads,
        compiler_params=pltpu.CompilerParams(vmem_limit_bytes=20 * MIB),
        cost_estimate=pl.CostEstimate(flops=MIB, bytes_accessed=MIB, transcendentals=0),
        name="up_sum" if up else "pre_sum",
    )(at, x, x_other, w, w_other)
    return in_pairs(outs)


def first_kernel(*refs):
    for p in range(3):
        for n in range(2):
            keep, came = refs[p * 4 + n * 2], refs[p * 4 + n * 2 + 1]
            total = keep[...] + came[...].astype(F32)
            refs[12 + p * 2][n] = total[:128]
            refs[13 + p * 2][n] = total[128:].astype(BF16)


def second_kernel(*refs):
    for p in range(3):
        total = refs[p * 2][...] + refs[p * 2 + 1][...].astype(F32)
        refs[6 + p * 2][...] = total
        refs[7 + p * 2][...] = total.astype(BF16)


def third_kernel(*refs):
    for p in range(3):
        keep, came, out = refs[p * 2], refs[p * 2 + 1], refs[6 + p]
        for block in range(2):
            mine, theirs = slice(block * 64, block * 64 + 64), slice(64 - block * 64, 128 - block * 64)
            for first in range(0, out.shape[2], 128):
                cols = slice(first, first + 128)
                up = keep[0, mine, cols] + came[0, theirs, cols].astype(F32)
                v = keep[1, mine, cols] + came[1, theirs, cols].astype(F32)
                square = v * v
                t = jnp.tanh(SLOPE * v * (1.0 + CUBE * square))
                half = 0.5 * (1.0 + t)
                out[1, mine, cols] = (v * half).astype(BF16)
                bend = 0.5 * SLOPE * v * (1.0 - t * t) * (1.0 + 3.0 * CUBE * square)
                out[0, mine, cols] = (up * (half + bend)).astype(BF16)


SLOPE, CUBE = 0.7978845608028654, 0.044715


def joint(kernel, name, arrays, shapes):
    outs = pl.pallas_call(
        kernel,
        in_specs=[pl.BlockSpec(memory_space=pltpu.VMEM)] * len(arrays),
        out_specs=[pl.BlockSpec(memory_space=pltpu.VMEM)] * len(shapes),
        out_shape=[jax.ShapeDtypeStruct(*shape) for shape in shapes],
        compiler_params=pltpu.CompilerParams(vmem_limit_bytes=16 * MIB),
        cost_estimate=pl.CostEstimate(flops=MIB, bytes_accessed=MIB, transcendentals=0),
        name=name,
    )(*arrays)
    return list(outs)


def gate_kernel(x, after, out):
    pass


def gate(x, after):
    anywhere = pl.BlockSpec(memory_space=pl.ANY)
    return pl.pallas_call(
        gate_kernel,
        in_specs=[anywhere] * 2,
        out_specs=anywhere,
        out_shape=jax.ShapeDtypeStruct(x.shape, x.dtype),
        input_output_aliases={0: 0},
        cost_estimate=pl.CostEstimate(flops=MIB, bytes_accessed=MIB, transcendentals=0),
        compiler_params=pltpu.CompilerParams(vmem_limit_bytes=MIB),
        name="gate",
    )(x, after)


def exchange_sums(up, pre):
    widths = [CUTS[p + 1] - CUTS[p] for p in range(3)]
    arrays = []
    for p, order in enumerate(ORDERS):
        for keep, send in (up[p], pre[p]):
            arrays += [keep, swap(send, order[0])]
    pair = [((2, 128, width), dtype) for width in widths for dtype in (F32, BF16)]
    left = joint(first_kernel, "first_sums", arrays, pair)
    for p, order in enumerate(ORDERS):
        left[p * 2 + 1] = swap(left[p * 2 + 1], order[1])
    left = joint(second_kernel, "second_sums", left, pair)
    for p, order in enumerate(ORDERS):
        left[p * 2 + 1] = swap(left[p * 2 + 1], order[2])
    return joint(third_kernel, "third_sums", left, [((2, 128, width), BF16) for width in widths])


def fourth_kernel(*refs):
    for p in range(3):
        for k in range(2):
            refs[6 + p][k] = refs[p * 2 + k][...]


def gather(parts):
    arrays = []
    for x, order in zip(parts, ORDERS):
        arrays += [x, swap(x, order[1])]
    held = joint(fourth_kernel, "fourth_blocks", arrays, [((2, *x.shape), BF16) for x in parts])
    pieces = []
    for x, order in zip(held, ORDERS):
        pieces += [x, swap(x, order[0])]
    return pieces


def back_part(at, pieces, w, half, total):
    for p, order in enumerate(ORDERS):
        rows = None
        width = CUTS[p + 1] - CUTS[p]
        for h in range(2):
            base = (at[1] if h == 0 else 1 - at[1]) * 2048 + CUTS[p]
            piece = pieces[h * 3 + p][:, 0].reshape(256, width)
            cols = w[:, pl.ds(pl.multiple_of(base, 256), width)]
            part = lax.dot_general(piece, cols, (((1,), (1,)), ((), ())), preferred_element_type=F32)
            rows = part if rows is None else rows + part
        for q, j in enumerate(places(order)[half * 4 : half * 4 + 4]):
            dst = pl.multiple_of(jnp.bitwise_xor(at[0], j) * 64, 64)
            total[pl.ds(dst, 64), :] += rows[q * 64 : (q + 1) * 64]


def held_kernel(at, *refs):
    pieces, w, total = refs[:6], refs[6], refs[7]
    total[...] = jnp.zeros_like(total)
    back_part(at, pieces, w, 0, total)


def came_kernel(at, *refs):
    pieces, w, before, out, total = refs[:6], refs[6], refs[7], refs[8], refs[9]
    total[...] = before[...]
    back_part(at, pieces, w, 1, total)
    low = lower((64, 8, 128))
    c = [total[:, k * 128 : (k + 1) * 128].reshape(64, 8, 128) for k in range(4)]
    r = [pltpu.roll(v, 4, 1) for v in c]
    for t in range(2):
        tile = slice(t * 8, t * 8 + 8)
        out[:, 0, tile] = jnp.where(low, c[2 * t], r[2 * t + 1]).astype(BF16)
        out[:, 1, tile] = jnp.where(low, r[2 * t], c[2 * t + 1]).astype(BF16)


def back_messages(at, pieces, w_in):
    vmem = pl.BlockSpec(memory_space=pltpu.VMEM)
    settings = dict(
        out_specs=vmem,
        compiler_params=pltpu.CompilerParams(vmem_limit_bytes=20 * MIB),
        cost_estimate=pl.CostEstimate(flops=512 * 512 * 4096, bytes_accessed=4 * MIB, transcendentals=0),
    )
    held, came = [[pieces[h * 6 + p * 2 + k] for h in range(2) for p in range(3)] for k in range(2)]
    total = pl.pallas_call(
        held_kernel,
        in_specs=[SCALARS] + [vmem] * 7,
        out_shape=jax.ShapeDtypeStruct((512, 512), F32),
        name="back_held",
        **settings,
    )(at, *held, w_in)
    return pl.pallas_call(
        came_kernel,
        in_specs=[SCALARS] + [vmem] * 8,
        out_shape=pltpu.HBM((64, 2, 16, 128), BF16),
        scratch_shapes=[pltpu.VMEM((512, 512), F32)],
        name="back_messages",
        **settings,
    )(at, *came, w_in, total)


def grads_kernel(at, *refs):
    pieces, (x, cot, grad_in, grad_out), scratch = refs[:12], refs[12:16], refs[16:]
    held, rows, turned, wide_in, wide_out, loads, stores = scratch
    todo = [(p, h) for p in range(3) for h in range(2)]
    arrivals = {}
    for p, h in todo:
        for which in range(2):
            for k in range(2):
                n = h * 6 + p * 2 + k
                target = held.at[which, h * 3 + p, k, :, :, 0 : CUTS[p + 1] - CUTS[p]]
                copy = pltpu.make_async_copy(pieces[n].at[:, which], target, loads.at[which * 12 + n])
                copy.start()
                arrivals[which, h, p, k] = copy
    rows_kernel(x, rows)
    dims = (((0,), (0,)), ((), ()))
    leaving = []

    def send(buffer, target):
        leaving.append(pltpu.make_async_copy(buffer, target, stores.at[len(leaving)]))
        leaving[-1].start()

    for p, h in todo:
        if h == 0:
            for q, j in enumerate(places(ORDERS[p])):
                src = pl.multiple_of(jnp.bitwise_xor(at[0], j) * 64, 64)
                turned[0, q * 64 : (q + 1) * 64, :] = rows[pl.ds(src, 64), :]
                turned[1, q * 64 : (q + 1) * 64, :] = cot[pl.ds(src, 64), :]
        for which in range(2):
            for k in range(2):
                arrivals[which, h, p, k].wait()
            for first in range(0, CUTS[p + 1] - CUTS[p], 256):
                piece = held[which, h * 3 + p, :, :, :, first : first + 256].reshape(512, 256)
                slot = (h * 2048 + CUTS[p] + first) // 256
                base = (at[1] if h == 0 else 1 - at[1]) * 2048 + CUTS[p] + first
                span = pl.ds(pl.multiple_of(base, 256), 256)
                if which == 0:
                    wide_in[slot] = lax.dot_general(turned[0], piece, dims, preferred_element_type=F32)
                    send(wide_in.at[slot], grad_in.at[:, span])
                else:
                    wide_out[slot] = lax.dot_general(piece, turned[1], dims, preferred_element_type=F32)
                    send(wide_out.at[slot], grad_out.at[span, :])
    for copy in leaving:
        copy.wait()


def grads_of(at, pieces, x, cot):
    anywhere, vmem = pl.BlockSpec(memory_space=pl.ANY), pl.BlockSpec(memory_space=pltpu.VMEM)
    pieces = [pltpu.with_memory_space_constraint(p, pltpu.HBM) for p in pieces]
    return pl.pallas_call(
        grads_kernel,
        in_specs=[SCALARS] + [anywhere] * 12 + [vmem] * 2,
        out_specs=[anywhere] * 2,
        out_shape=[pltpu.HBM((512, 4096), F32), pltpu.HBM((4096, 512), F32)],
        scratch_shapes=[
            pltpu.VMEM((2, 6, 2, 2, 128, 768), BF16),
            pltpu.VMEM((512, 512), BF16),
            pltpu.VMEM((2, 512, 512), BF16),
            pltpu.VMEM((16, 512, 256), F32),
            pltpu.VMEM((16, 256, 512), F32),
            pltpu.SemaphoreType.DMA((24,)),
            pltpu.SemaphoreType.DMA((32,)),
        ],
        compiler_params=pltpu.CompilerParams(vmem_limit_bytes=36 * MIB),
        cost_estimate=pl.CostEstimate(flops=4 * 512 * 512 * 4096, bytes_accessed=24 * MIB, transcendentals=0),
        name="grads",
    )(at, *pieces, x, cot)


def act_kernel(x, act, gain, out, twice, back):
    a = act[...].astype(F32)
    twice[0:4, :] = a
    twice[4:8, :] = a
    a = twice[...]
    center = a - jnp.mean(a, axis=1, keepdims=True)
    inverse = lax.rsqrt(jnp.mean(center * center, axis=1, keepdims=True) + EPSILON)
    scaled = center * inverse
    low = lower((8, 128))
    for g in range(16):
        total = x[g // 8 * 64 + g % 8].astype(F32)
        for d in range(1, 8):
            total += x[g // 8 * 64 + d * 8 + g % 8].astype(F32)
        for t in range(2):
            tile = total[t * 8 : t * 8 + 8]
            turned = pltpu.roll(tile, 4, 0)
            at = g * 512 + t * 256
            back[:, at : at + 128] = jnp.where(low, tile, turned)
            back[:, at + 128 : at + 256] = jnp.where(low, turned, tile)
    dxhat = back[...] * gain[...]
    first = jnp.mean(dxhat, axis=1, keepdims=True)
    second = jnp.mean(dxhat * scaled, axis=1, keepdims=True)
    back[...] = inverse * (dxhat - first - scaled * second)
    out[...] = back[0:4, :]


def grad_act_of(x, act, gain):
    return pl.pallas_call(
        act_kernel,
        in_specs=[pl.BlockSpec(memory_space=pltpu.VMEM)] * 3,
        out_specs=pl.BlockSpec(memory_space=pltpu.VMEM),
        out_shape=jax.ShapeDtypeStruct((4, 8192), F32),
        scratch_shapes=[pltpu.VMEM((8, 8192), F32), pltpu.VMEM((8, 8192), F32)],
        compiler_params=pltpu.CompilerParams(vmem_limit_bytes=8 * MIB),
        name="grad_act",
    )(x, act, gain.reshape(1, -1))


def local(act, gain, shift, w_in, w_out, cotangent):
    section, tensor = lax.axis_index("section"), lax.axis_index("tensor")
    core, ring = lax.bitwise_and(tensor, 1), lax.shift_right_logical(tensor, 1)
    bit_a = jnp.where((ring == 1) | (ring == 2), 1, 0)
    number = bit_a * 4 + lax.bitwise_and(ring, 2) + section
    at = jnp.stack([number, core]).astype(jnp.int32)

    out_other = swap(w_out, "core")
    cot_other = swap(cotangent, "core")
    in_other = swap(w_in, "core")
    messages = norm_messages(act, gain, shift)
    mixed = lax.all_to_all(messages.reshape(128, 16, 128), EVERY, 0, 0, tiled=True)
    up = chip_sum(at, cotangent, cot_other, w_out, out_other, True)
    mixed = gate(mixed, up[0][0])
    mixed_other = swap(mixed, "core")
    pre = chip_sum(at, mixed, mixed_other, w_in, in_other, False)
    pieces = gather(exchange_sums(up, pre))
    pieces += [swap(p, "core") for p in pieces]

    share = back_messages(at, pieces, w_in)
    returned = lax.all_to_all(share.reshape(128, 16, 128), EVERY, 0, 0, tiled=True)
    grad_act = grad_act_of(returned, act, gain)
    grad_in, grad_out = grads_of(at, pieces, mixed, cotangent)
    return (grad_in, grad_out, grad_act)


def solution(mesh):
    in_specs = (
        P(EVERY, None),
        P(),
        P(),
        P(OWNERS, "dp"),
        P("dp", OWNERS),
        P(None, OWNERS),
    )
    out_specs = (P(OWNERS, "dp"), P("dp", OWNERS), P(EVERY, None))
    return jax.shard_map(local, mesh=mesh, in_specs=in_specs, out_specs=out_specs, check_vma=False)
```

```python
import functools

import jax
import jax.numpy as jnp
from jax import lax
from jax.experimental import pallas as pl
from jax.experimental.pallas import tpu as pltpu
from jax.sharding import PartitionSpec as P

EPSILON = 1e-05
OWNERS = ("section", "tensor")
EVERY = ("section", "dp", "tensor")
BF16, F32 = jnp.bfloat16, jnp.float32
MIB = 1 << 20

def swap(x, link):
    pairs = []
    for s in range(2):
        for y in range(4):
            for c in range(2):
                if link == "core":
                    s2, y2, c2 = s, y, 1 - c
                else:
                    y2 = y ^ 1 if link & 4 else y
                    y2 = 3 - y2 if link & 2 else y2
                    s2, c2 = s ^ (link & 1), c
                pairs.append((s * 8 + y * 2 + c, s2 * 8 + y2 * 2 + c2))
    return lax.ppermute(x, OWNERS, pairs)


def lower(shape):
    return lax.broadcasted_iota(jnp.int32, shape, len(shape) - 2) % 8 < 4


SCALARS = pl.BlockSpec(memory_space=pltpu.SMEM)


def norm_kernel(act, gain, shift, out, twice):
    x = act[...].astype(F32)
    twice[0:4, :] = x
    twice[4:8, :] = x
    x = twice[...]
    center = x - jnp.mean(x, axis=1, keepdims=True)
    inverse = lax.rsqrt(jnp.mean(center * center, axis=1, keepdims=True) + EPSILON)
    twice[...] = center * inverse * gain[...] + shift[...]
    low = lower((8, 128))
    for g in range(16):
        cols = [twice[:, g * 512 + k * 128 : g * 512 + (k + 1) * 128] for k in range(4)]
        piece = jnp.concatenate([jnp.where(low, cols[0], cols[1]), jnp.where(low, cols[2], cols[3])], axis=0)
        piece = piece.astype(BF16)
        for d in range(8):
            out[g // 8, d, g % 8] = piece


def norm_messages(act, gain, shift):
    return pl.pallas_call(
        norm_kernel,
        out_shape=pltpu.HBM((2, 8, 8, 16, 128), BF16),
        scratch_shapes=[pltpu.VMEM((8, 8192), F32)],
        compiler_params=pltpu.CompilerParams(vmem_limit_bytes=56 * MIB),
        name="norm_messages",
    )(act, gain.reshape(1, -1), shift.reshape(1, -1))


def unfold(even, odd, k, low):
    tile = slice(k // 2 * 8, k // 2 * 8 + 8)
    e, o = even[:, tile], odd[:, tile]
    if k % 2 == 0:
        return jnp.where(low, e, pltpu.roll(o, 4, 1))
    return jnp.where(low, pltpu.roll(e, 4, 1), o)


def rows_kernel(x, out):
    x = x[...].reshape(64, 2, 16, 128)
    even, odd = x[:, 0].astype(F32), x[:, 1].astype(F32)
    low = lower((64, 8, 128))
    for k in range(4):
        out[:, k * 128 : (k + 1) * 128] = unfold(even, odd, k, low).reshape(512, 128).astype(BF16)


ORDERS = ((4, 2, 1), (2, 1, 4), (1, 4, 2))
CUTS = (0, 768, 1536, 2048)


def places(order):
    return [sum(link for k, link in enumerate(order) if q >> (2 - k) & 1) for q in range(8)]


def split(total, first_column, outs):
    last_column = first_column + total.shape[1]
    for p, order in enumerate(ORDERS):
        first, last = max(CUTS[p], first_column), min(CUTS[p + 1], last_column)
        if first >= last:
            continue
        for q, j in enumerate(places(order)):
            out = outs[p * 2 + q // 4]
            block = total[j * 64 : (j + 1) * 64, first - first_column : last - first_column]
            out[q % 4 * 64 : (q % 4 + 1) * 64, first - CUTS[p] : last - CUTS[p]] = block.astype(out.dtype)


def up_kernel(at, x, x_other, w, w_other, *refs):
    outs, (lhs, weights, loads) = refs[:6], refs[6:]
    span = pl.ds(pl.multiple_of(at[1] * 2048, 2048), 2048)
    copies = []
    for n, ref in enumerate((w, w_other)):
        copies.append(pltpu.make_async_copy(ref.at[span, :], weights.at[:, n * 512 : n * 512 + 512], loads.at[n]))
        copies[n].start()
    for j in range(8):
        src = pl.multiple_of(jnp.bitwise_xor(at[0], j) * 64, 64)
        lhs[j * 64 : (j + 1) * 64, 0:512] = x[pl.ds(src, 64), :]
        lhs[j * 64 : (j + 1) * 64, 512:1024] = x_other[pl.ds(src, 64), :]
    for copy in copies:
        copy.wait()
    for first in (0, 1024):
        dims = (((1,), (1,)), ((), ()))
        split(lax.dot_general(lhs[...], weights[first : first + 1024], dims, preferred_element_type=F32), first, outs)


def pre_kernel(at, x, x_other, w, w_other, *refs):
    outs, (lhs, weights, tokens, loads, token_loads) = refs[:6], refs[6:]
    copies = [pltpu.make_async_copy(ref, tokens.at[n], token_loads.at[n]) for n, ref in enumerate((x, x_other))]
    for k in range(2):
        for n, ref in enumerate((w, w_other)):
            source = ref.at[:, pl.ds(pl.multiple_of(at[1] * 2048 + k * 1024, 1024), 1024)]
            target = weights.at[n * 512 : n * 512 + 512, k * 1024 : k * 1024 + 1024]
            copies.append(pltpu.make_async_copy(source, target, loads.at[k * 2 + n]))
    for copy in copies:
        copy.start()
    low = lower((8, 8, 128))
    for n in range(2):
        copies[n].wait()
        for j in range(8):
            some = tokens[n, pl.ds(jnp.bitwise_xor(at[0], j) * 16, 16)].reshape(8, 2, 16, 128)
            even, odd = some[:, 0].astype(F32), some[:, 1].astype(F32)
            for k in range(4):
                rows = unfold(even, odd, k, low).reshape(64, 128).astype(BF16)
                lhs[j * 64 : (j + 1) * 64, n * 512 + k * 128 : n * 512 + (k + 1) * 128] = rows
    for k in range(2):
        copies[2 + 2 * k].wait()
        copies[3 + 2 * k].wait()
        split(jnp.dot(lhs[...], weights[:, k * 1024 : k * 1024 + 1024], preferred_element_type=F32), k * 1024, outs)


HALVES = [
    jax.ShapeDtypeStruct((256, CUTS[p + 1] - CUTS[p]), dtype) for p in range(3) for dtype in (F32, BF16)
]
VMEM_BLOCK, ANY_BLOCK = pl.BlockSpec(memory_space=pltpu.VMEM), pl.BlockSpec(memory_space=pl.ANY)


def in_pairs(arrays):
    return [(arrays[2 * p], arrays[2 * p + 1]) for p in range(3)]


def chip_sum(at, x, x_other, w, w_other, up):
    w, w_other = [pltpu.with_memory_space_constraint(v, pltpu.HBM) for v in (w, w_other)]
    scratch = [pltpu.VMEM((512, 1024), BF16), pltpu.VMEM((2048, 1024) if up else (1024, 2048), BF16)]
    loads = [pltpu.SemaphoreType.DMA((2,))]
    if not up:
        scratch.append(pltpu.VMEM((2, 128, 16, 128), BF16))
        loads.insert(0, pltpu.SemaphoreType.DMA((4,)))
    outs = pl.pallas_call(
        up_kernel if up else pre_kernel,
        in_specs=[SCALARS] + [VMEM_BLOCK if up else ANY_BLOCK] * 2 + [ANY_BLOCK] * 2,
        out_specs=[VMEM_BLOCK] * 6,
        out_shape=HALVES,
        scratch_shapes=scratch + loads,
        compiler_params=pltpu.CompilerParams(vmem_limit_bytes=20 * MIB),
        cost_estimate=pl.CostEstimate(flops=MIB, bytes_accessed=MIB, transcendentals=0),
        name="up_sum" if up else "pre_sum",
    )(at, x, x_other, w, w_other)
    return in_pairs(outs)


def first_kernel(*refs):
    for p in range(3):
        for n in range(2):
            keep, came = refs[p * 4 + n * 2], refs[p * 4 + n * 2 + 1]
            total = keep[...] + came[...].astype(F32)
            refs[12 + p * 2][n] = total[:128]
            refs[13 + p * 2][n] = total[128:].astype(BF16)


def second_kernel(*refs):
    for p in range(3):
        total = refs[p * 2][...] + refs[p * 2 + 1][...].astype(F32)
        refs[6 + p * 2][...] = total
        refs[7 + p * 2][...] = total.astype(BF16)


def third_kernel(*refs):
    for p in range(3):
        keep, came, out = refs[p * 2], refs[p * 2 + 1], refs[6 + p]
        for block in range(2):
            mine, theirs = slice(block * 64, block * 64 + 64), slice(64 - block * 64, 128 - block * 64)
            for first in range(0, out.shape[2], 128):
                cols = slice(first, first + 128)
                up = keep[0, mine, cols] + came[0, theirs, cols].astype(F32)
                v = keep[1, mine, cols] + came[1, theirs, cols].astype(F32)
                square = v * v
                t = jnp.tanh(SLOPE * v * (1.0 + CUBE * square))
                half = 0.5 * (1.0 + t)
                out[1, mine, cols] = (v * half).astype(BF16)
                bend = 0.5 * SLOPE * v * (1.0 - t * t) * (1.0 + 3.0 * CUBE * square)
                out[0, mine, cols] = (up * (half + bend)).astype(BF16)


SLOPE, CUBE = 0.7978845608028654, 0.044715


def joint(kernel, name, arrays, shapes, step):
    each = len(arrays) // 3
    picked = [p * each + k for p in far_first(step) for k in range(each)]

    def body(*refs):
        inputs = [None] * len(picked)
        for place, source in enumerate(picked):
            inputs[source] = refs[place]
        kernel(*inputs, *refs[len(picked) :])

    outs = pl.pallas_call(
        body,
        in_specs=[pl.BlockSpec(memory_space=pltpu.VMEM)] * len(arrays),
        out_specs=[pl.BlockSpec(memory_space=pltpu.VMEM)] * len(shapes),
        out_shape=[jax.ShapeDtypeStruct(*shape) for shape in shapes],
        compiler_params=pltpu.CompilerParams(vmem_limit_bytes=16 * MIB),
        cost_estimate=pl.CostEstimate(flops=MIB, bytes_accessed=MIB, transcendentals=0),
        name=name,
    )(*[arrays[k] for k in picked])
    return list(outs)


def gate_kernel(x, after, out):
    pass


def gate(x, after):
    anywhere = pl.BlockSpec(memory_space=pl.ANY)
    return pl.pallas_call(
        gate_kernel,
        in_specs=[anywhere] * 2,
        out_specs=anywhere,
        out_shape=jax.ShapeDtypeStruct(x.shape, x.dtype),
        input_output_aliases={0: 0},
        cost_estimate=pl.CostEstimate(flops=MIB, bytes_accessed=MIB, transcendentals=0),
        compiler_params=pltpu.CompilerParams(vmem_limit_bytes=MIB),
        name="gate",
    )(x, after)


def far_first(step):
    return sorted(range(3), key=lambda p: ORDERS[p][step] != 1)


def exchange_sums(up, pre):
    widths = [CUTS[p + 1] - CUTS[p] for p in range(3)]
    arrays = [None] * 12
    for n, sums in enumerate((up, pre)):
        for p in far_first(0):
            keep, send = sums[p]
            arrays[p * 4 + n * 2 : p * 4 + n * 2 + 2] = keep, swap(send, ORDERS[p][0])
    pair = [((2, 128, width), dtype) for width in widths for dtype in (F32, BF16)]
    left = joint(first_kernel, "first_sums", arrays, pair, 0)
    for p in far_first(1):
        left[p * 2 + 1] = swap(left[p * 2 + 1], ORDERS[p][1])
    left = joint(second_kernel, "second_sums", left, pair, 1)
    for p in far_first(2):
        left[p * 2 + 1] = swap(left[p * 2 + 1], ORDERS[p][2])
    return joint(third_kernel, "third_sums", left, [((2, 128, width), BF16) for width in widths], 2)


def fourth_kernel(*refs):
    for p in range(3):
        for k in range(2):
            refs[6 + p][k] = refs[p * 2 + k][...]


def gather(parts):
    arrays = [None] * 6
    for p in far_first(1):
        arrays[p * 2 : p * 2 + 2] = parts[p], swap(parts[p], ORDERS[p][1])
    held = joint(fourth_kernel, "fourth_blocks", arrays, [((2, *x.shape), BF16) for x in parts], 1)
    pieces = [None] * 6
    for p in far_first(0):
        pieces[p * 2 : p * 2 + 2] = held[p], swap(held[p], ORDERS[p][0])
    return pieces


def back_part(at, pieces, w, half, total):
    for p, order in enumerate(ORDERS):
        rows = None
        width = CUTS[p + 1] - CUTS[p]
        for h in range(2):
            base = (at[1] if h == 0 else 1 - at[1]) * 2048 + CUTS[p]
            piece = pieces[h * 3 + p][:, 0].reshape(256, width)
            cols = w[:, pl.ds(pl.multiple_of(base, 256), width)]
            part = lax.dot_general(piece, cols, (((1,), (1,)), ((), ())), preferred_element_type=F32)
            rows = part if rows is None else rows + part
        for q, j in enumerate(places(order)[half * 4 : half * 4 + 4]):
            dst = pl.multiple_of(jnp.bitwise_xor(at[0], j) * 64, 64)
            total[pl.ds(dst, 64), :] += rows[q * 64 : (q + 1) * 64]


def held_kernel(at, *refs):
    pieces, w, total = refs[:6], refs[6], refs[7]
    total[...] = jnp.zeros_like(total)
    back_part(at, pieces, w, 0, total)


def came_kernel(at, *refs):
    pieces, w, before, out, total = refs[:6], refs[6], refs[7], refs[8], refs[9]
    total[...] = before[...]
    back_part(at, pieces, w, 1, total)
    low = lower((64, 8, 128))
    c = [total[:, k * 128 : (k + 1) * 128].reshape(64, 8, 128) for k in range(4)]
    r = [pltpu.roll(v, 4, 1) for v in c]
    for t in range(2):
        tile = slice(t * 8, t * 8 + 8)
        out[:, 0, tile] = jnp.where(low, c[2 * t], r[2 * t + 1]).astype(BF16)
        out[:, 1, tile] = jnp.where(low, r[2 * t], c[2 * t + 1]).astype(BF16)


def back_messages(at, pieces, w_in):
    vmem = pl.BlockSpec(memory_space=pltpu.VMEM)
    settings = dict(
        out_specs=vmem,
        compiler_params=pltpu.CompilerParams(vmem_limit_bytes=20 * MIB),
        cost_estimate=pl.CostEstimate(flops=512 * 512 * 4096, bytes_accessed=4 * MIB, transcendentals=0),
    )
    held, came = [[pieces[h * 6 + p * 2 + k] for h in range(2) for p in range(3)] for k in range(2)]
    total = pl.pallas_call(
        held_kernel,
        in_specs=[SCALARS] + [vmem] * 7,
        out_shape=jax.ShapeDtypeStruct((512, 512), F32),
        name="back_held",
        **settings,
    )(at, *held, w_in)
    return pl.pallas_call(
        came_kernel,
        in_specs=[SCALARS] + [vmem] * 8,
        out_shape=pltpu.HBM((64, 2, 16, 128), BF16),
        scratch_shapes=[pltpu.VMEM((512, 512), F32)],
        name="back_messages",
        **settings,
    )(at, *came, w_in, total)


def grads_kernel(at, *refs):
    pieces, (x, cot, grad_in, grad_out), scratch = refs[:12], refs[12:16], refs[16:]
    held, rows, turned, wide_in, wide_out, loads, stores = scratch
    todo = [(p, h) for p in range(3) for h in range(2)]
    arrivals = {}
    for p, h in todo:
        for which in range(2):
            for k in range(2):
                n = h * 6 + p * 2 + k
                target = held.at[which, h * 3 + p, k, :, :, 0 : CUTS[p + 1] - CUTS[p]]
                copy = pltpu.make_async_copy(pieces[n].at[:, which], target, loads.at[which * 12 + n])
                copy.start()
                arrivals[which, h, p, k] = copy
    rows_kernel(x, rows)
    dims = (((0,), (0,)), ((), ()))
    leaving = []

    def send(buffer, target):
        leaving.append(pltpu.make_async_copy(buffer, target, stores.at[len(leaving)]))
        leaving[-1].start()

    for p, h in todo:
        if h == 0:
            for q, j in enumerate(places(ORDERS[p])):
                src = pl.multiple_of(jnp.bitwise_xor(at[0], j) * 64, 64)
                turned[0, q * 64 : (q + 1) * 64, :] = rows[pl.ds(src, 64), :]
                turned[1, q * 64 : (q + 1) * 64, :] = cot[pl.ds(src, 64), :]
        for which in range(2):
            for k in range(2):
                arrivals[which, h, p, k].wait()
            for first in range(0, CUTS[p + 1] - CUTS[p], 256):
                piece = held[which, h * 3 + p, :, :, :, first : first + 256].reshape(512, 256)
                slot = (h * 2048 + CUTS[p] + first) // 256
                base = (at[1] if h == 0 else 1 - at[1]) * 2048 + CUTS[p] + first
                span = pl.ds(pl.multiple_of(base, 256), 256)
                if which == 0:
                    wide_in[slot] = lax.dot_general(turned[0], piece, dims, preferred_element_type=F32)
                    send(wide_in.at[slot], grad_in.at[:, span])
                else:
                    wide_out[slot] = lax.dot_general(piece, turned[1], dims, preferred_element_type=F32)
                    send(wide_out.at[slot], grad_out.at[span, :])
    for copy in leaving:
        copy.wait()


def grads_of(at, pieces, x, cot):
    anywhere, vmem = pl.BlockSpec(memory_space=pl.ANY), pl.BlockSpec(memory_space=pltpu.VMEM)
    pieces = [pltpu.with_memory_space_constraint(p, pltpu.HBM) for p in pieces]
    return pl.pallas_call(
        grads_kernel,
        in_specs=[SCALARS] + [anywhere] * 12 + [vmem] * 2,
        out_specs=[anywhere] * 2,
        out_shape=[pltpu.HBM((512, 4096), F32), pltpu.HBM((4096, 512), F32)],
        scratch_shapes=[
            pltpu.VMEM((2, 6, 2, 2, 128, 768), BF16),
            pltpu.VMEM((512, 512), BF16),
            pltpu.VMEM((2, 512, 512), BF16),
            pltpu.VMEM((16, 512, 256), F32),
            pltpu.VMEM((16, 256, 512), F32),
            pltpu.SemaphoreType.DMA((24,)),
            pltpu.SemaphoreType.DMA((32,)),
        ],
        compiler_params=pltpu.CompilerParams(vmem_limit_bytes=36 * MIB),
        cost_estimate=pl.CostEstimate(flops=4 * 512 * 512 * 4096, bytes_accessed=24 * MIB, transcendentals=0),
        name="grads",
    )(at, *pieces, x, cot)


def act_kernel(x, act, gain, out, twice, back):
    a = act[...].astype(F32)
    twice[0:4, :] = a
    twice[4:8, :] = a
    a = twice[...]
    center = a - jnp.mean(a, axis=1, keepdims=True)
    inverse = lax.rsqrt(jnp.mean(center * center, axis=1, keepdims=True) + EPSILON)
    scaled = center * inverse
    low = lower((8, 128))
    for g in range(16):
        total = x[g // 8 * 64 + g % 8].astype(F32)
        for d in range(1, 8):
            total += x[g // 8 * 64 + d * 8 + g % 8].astype(F32)
        for t in range(2):
            tile = total[t * 8 : t * 8 + 8]
            turned = pltpu.roll(tile, 4, 0)
            at = g * 512 + t * 256
            back[:, at : at + 128] = jnp.where(low, tile, turned)
            back[:, at + 128 : at + 256] = jnp.where(low, turned, tile)
    dxhat = back[...] * gain[...]
    first = jnp.mean(dxhat, axis=1, keepdims=True)
    second = jnp.mean(dxhat * scaled, axis=1, keepdims=True)
    back[...] = inverse * (dxhat - first - scaled * second)
    out[...] = back[0:4, :]


def grad_act_of(x, act, gain):
    return pl.pallas_call(
        act_kernel,
        in_specs=[pl.BlockSpec(memory_space=pltpu.VMEM)] * 3,
        out_specs=pl.BlockSpec(memory_space=pltpu.VMEM),
        out_shape=jax.ShapeDtypeStruct((4, 8192), F32),
        scratch_shapes=[pltpu.VMEM((8, 8192), F32), pltpu.VMEM((8, 8192), F32)],
        compiler_params=pltpu.CompilerParams(vmem_limit_bytes=8 * MIB),
        name="grad_act",
    )(x, act, gain.reshape(1, -1))


def local(act, gain, shift, w_in, w_out, cotangent):
    section, tensor = lax.axis_index("section"), lax.axis_index("tensor")
    core, ring = lax.bitwise_and(tensor, 1), lax.shift_right_logical(tensor, 1)
    bit_a = jnp.where((ring == 1) | (ring == 2), 1, 0)
    number = bit_a * 4 + lax.bitwise_and(ring, 2) + section
    at = jnp.stack([number, core]).astype(jnp.int32)

    out_other = swap(w_out, "core")
    cot_other = swap(cotangent, "core")
    in_other = swap(w_in, "core")
    messages = norm_messages(act, gain, shift)
    mixed = lax.all_to_all(messages.reshape(128, 16, 128), EVERY, 0, 0, tiled=True)
    up = chip_sum(at, cotangent, cot_other, w_out, out_other, True)
    mixed = gate(mixed, up[0][0])
    mixed_other = swap(mixed, "core")
    pre = chip_sum(at, mixed, mixed_other, w_in, in_other, False)
    pieces = gather(exchange_sums(up, pre))
    pieces += [swap(p, "core") for p in pieces]

    share = back_messages(at, pieces, w_in)
    returned = lax.all_to_all(share.reshape(128, 16, 128), EVERY, 0, 0, tiled=True)
    grad_act = grad_act_of(returned, act, gain)
    grad_in, grad_out = grads_of(at, pieces, mixed, cotangent)
    return (grad_in, grad_out, grad_act)


def solution(mesh):
    in_specs = (
        P(EVERY, None),
        P(),
        P(),
        P(OWNERS, "dp"),
        P("dp", OWNERS),
        P(None, OWNERS),
    )
    out_specs = (P(OWNERS, "dp"), P("dp", OWNERS), P(EVERY, None))
    return jax.shard_map(local, mesh=mesh, in_specs=in_specs, out_specs=out_specs, check_vma=False)
```

```python
import functools

import jax
import jax.numpy as jnp
from jax import lax
from jax.experimental import pallas as pl
from jax.experimental.pallas import tpu as pltpu
from jax.sharding import PartitionSpec as P

EPSILON = 1e-05
OWNERS = ("section", "tensor")
EVERY = ("section", "dp", "tensor")
BF16, F32 = jnp.bfloat16, jnp.float32
MIB = 1 << 20

def swap(x, link):
    pairs = []
    for s in range(2):
        for y in range(4):
            for c in range(2):
                if link == "core":
                    s2, y2, c2 = s, y, 1 - c
                else:
                    y2 = y ^ 1 if link & 4 else y
                    y2 = 3 - y2 if link & 2 else y2
                    s2, c2 = s ^ (link & 1), c
                pairs.append((s * 8 + y * 2 + c, s2 * 8 + y2 * 2 + c2))
    return lax.ppermute(x, OWNERS, pairs)


def lower(shape):
    return lax.broadcasted_iota(jnp.int32, shape, len(shape) - 2) % 8 < 4


SCALARS = pl.BlockSpec(memory_space=pltpu.SMEM)


def norm_kernel(act, gain, shift, out, twice):
    x = act[...].astype(F32)
    twice[0:4, :] = x
    twice[4:8, :] = x
    x = twice[...]
    center = x - jnp.mean(x, axis=1, keepdims=True)
    inverse = lax.rsqrt(jnp.mean(center * center, axis=1, keepdims=True) + EPSILON)
    twice[...] = center * inverse * gain[...] + shift[...]
    low = lower((8, 128))
    for g in range(16):
        cols = [twice[:, g * 512 + k * 128 : g * 512 + (k + 1) * 128] for k in range(4)]
        piece = jnp.concatenate([jnp.where(low, cols[0], cols[1]), jnp.where(low, cols[2], cols[3])], axis=0)
        piece = piece.astype(BF16)
        for d in range(8):
            out[g // 8, d, g % 8] = piece


def norm_messages(act, gain, shift):
    return pl.pallas_call(
        norm_kernel,
        out_shape=pltpu.HBM((2, 8, 8, 16, 128), BF16),
        scratch_shapes=[pltpu.VMEM((8, 8192), F32)],
        compiler_params=pltpu.CompilerParams(vmem_limit_bytes=56 * MIB),
        name="norm_messages",
    )(act, gain.reshape(1, -1), shift.reshape(1, -1))


def unfold(even, odd, k, low):
    tile = slice(k // 2 * 8, k // 2 * 8 + 8)
    e, o = even[:, tile], odd[:, tile]
    if k % 2 == 0:
        return jnp.where(low, e, pltpu.roll(o, 4, 1))
    return jnp.where(low, pltpu.roll(e, 4, 1), o)


def rows_kernel(x, out):
    x = x[...].reshape(64, 2, 16, 128)
    even, odd = x[:, 0].astype(F32), x[:, 1].astype(F32)
    low = lower((64, 8, 128))
    for k in range(4):
        out[:, k * 128 : (k + 1) * 128] = unfold(even, odd, k, low).reshape(512, 128).astype(BF16)


ORDERS = ((4, 2, 1), (2, 1, 4), (1, 4, 2))
CUTS = (0, 768, 1536, 2048)


def places(order):
    return [sum(link for k, link in enumerate(order) if q >> (2 - k) & 1) for q in range(8)]


def split(total, first_column, outs):
    last_column = first_column + total.shape[1]
    for p, order in enumerate(ORDERS):
        first, last = max(CUTS[p], first_column), min(CUTS[p + 1], last_column)
        if first >= last:
            continue
        for q, j in enumerate(places(order)):
            out = outs[p * 2 + q // 4]
            block = total[j * 64 : (j + 1) * 64, first - first_column : last - first_column]
            out[q % 4 * 64 : (q % 4 + 1) * 64, first - CUTS[p] : last - CUTS[p]] = block.astype(out.dtype)


def up_kernel(at, x, x_other, w, w_other, *refs):
    outs, (lhs, weights, loads) = refs[:6], refs[6:]
    span = pl.ds(pl.multiple_of(at[1] * 2048, 2048), 2048)
    copies = []
    for n, ref in enumerate((w, w_other)):
        copies.append(pltpu.make_async_copy(ref.at[span, :], weights.at[:, n * 512 : n * 512 + 512], loads.at[n]))
        copies[n].start()
    for j in range(8):
        src = pl.multiple_of(jnp.bitwise_xor(at[0], j) * 64, 64)
        lhs[j * 64 : (j + 1) * 64, 0:512] = x[pl.ds(src, 64), :]
        lhs[j * 64 : (j + 1) * 64, 512:1024] = x_other[pl.ds(src, 64), :]
    for copy in copies:
        copy.wait()
    for first in (0, 1024):
        dims = (((1,), (1,)), ((), ()))
        split(lax.dot_general(lhs[...], weights[first : first + 1024], dims, preferred_element_type=F32), first, outs)


def pre_kernel(at, x, x_other, w, w_other, *refs):
    outs, (lhs, weights, tokens, loads, token_loads) = refs[:6], refs[6:]
    copies = [pltpu.make_async_copy(ref, tokens.at[n], token_loads.at[n]) for n, ref in enumerate((x, x_other))]
    for k in range(2):
        for n, ref in enumerate((w, w_other)):
            source = ref.at[:, pl.ds(pl.multiple_of(at[1] * 2048 + k * 1024, 1024), 1024)]
            target = weights.at[n * 512 : n * 512 + 512, k * 1024 : k * 1024 + 1024]
            copies.append(pltpu.make_async_copy(source, target, loads.at[k * 2 + n]))
    for copy in copies:
        copy.start()
    low = lower((8, 8, 128))
    for n in range(2):
        copies[n].wait()
        for j in range(8):
            some = tokens[n, pl.ds(jnp.bitwise_xor(at[0], j) * 16, 16)].reshape(8, 2, 16, 128)
            even, odd = some[:, 0].astype(F32), some[:, 1].astype(F32)
            for k in range(4):
                rows = unfold(even, odd, k, low).reshape(64, 128).astype(BF16)
                lhs[j * 64 : (j + 1) * 64, n * 512 + k * 128 : n * 512 + (k + 1) * 128] = rows
    for k in range(2):
        copies[2 + 2 * k].wait()
        copies[3 + 2 * k].wait()
        split(jnp.dot(lhs[...], weights[:, k * 1024 : k * 1024 + 1024], preferred_element_type=F32), k * 1024, outs)


HALVES = [
    jax.ShapeDtypeStruct((256, CUTS[p + 1] - CUTS[p]), dtype) for p in range(3) for dtype in (F32, BF16)
]
VMEM_BLOCK, ANY_BLOCK = pl.BlockSpec(memory_space=pltpu.VMEM), pl.BlockSpec(memory_space=pl.ANY)


def in_pairs(arrays):
    return [(arrays[2 * p], arrays[2 * p + 1]) for p in range(3)]


def chip_sum(at, x, x_other, w, w_other, up):
    w, w_other = [pltpu.with_memory_space_constraint(v, pltpu.HBM) for v in (w, w_other)]
    scratch = [pltpu.VMEM((512, 1024), BF16), pltpu.VMEM((2048, 1024) if up else (1024, 2048), BF16)]
    loads = [pltpu.SemaphoreType.DMA((2,))]
    if not up:
        scratch.append(pltpu.VMEM((2, 128, 16, 128), BF16))
        loads.insert(0, pltpu.SemaphoreType.DMA((4,)))
    outs = pl.pallas_call(
        up_kernel if up else pre_kernel,
        in_specs=[SCALARS] + [VMEM_BLOCK if up else ANY_BLOCK] * 2 + [ANY_BLOCK] * 2,
        out_specs=[VMEM_BLOCK] * 6,
        out_shape=HALVES,
        scratch_shapes=scratch + loads,
        compiler_params=pltpu.CompilerParams(vmem_limit_bytes=20 * MIB),
        cost_estimate=pl.CostEstimate(flops=MIB, bytes_accessed=MIB, transcendentals=0),
        name="up_sum" if up else "pre_sum",
    )(at, x, x_other, w, w_other)
    return in_pairs(outs)


def first_kernel(*refs):
    for p in range(3):
        for n in range(2):
            keep, came = refs[p * 4 + n * 2], refs[p * 4 + n * 2 + 1]
            total = keep[...] + came[...].astype(F32)
            refs[12 + p * 2][n] = total[:128]
            refs[13 + p * 2][n] = total[128:].astype(BF16)


def second_kernel(*refs):
    for p in range(3):
        total = refs[p * 2][...] + refs[p * 2 + 1][...].astype(F32)
        refs[6 + p * 2][...] = total
        refs[7 + p * 2][...] = total.astype(BF16)


def third_kernel(*refs):
    for p in range(3):
        keep, came, out = refs[p * 2], refs[p * 2 + 1], refs[6 + p]
        for block in range(2):
            mine, theirs = slice(block * 64, block * 64 + 64), slice(64 - block * 64, 128 - block * 64)
            for first in range(0, out.shape[2], 128):
                cols = slice(first, first + 128)
                up = keep[0, mine, cols] + came[0, theirs, cols].astype(F32)
                v = keep[1, mine, cols] + came[1, theirs, cols].astype(F32)
                square = v * v
                t = jnp.tanh(SLOPE * v * (1.0 + CUBE * square))
                half = 0.5 * (1.0 + t)
                out[1, mine, cols] = (v * half).astype(BF16)
                bend = 0.5 * SLOPE * v * (1.0 - t * t) * (1.0 + 3.0 * CUBE * square)
                out[0, mine, cols] = (up * (half + bend)).astype(BF16)


SLOPE, CUBE = 0.7978845608028654, 0.044715


def joint(kernel, name, arrays, shapes, step):
    each = len(arrays) // 3
    picked = [p * each + k for p in far_first(step) for k in range(each)]

    def body(*refs):
        inputs = [None] * len(picked)
        for place, source in enumerate(picked):
            inputs[source] = refs[place]
        kernel(*inputs, *refs[len(picked) :])

    outs = pl.pallas_call(
        body,
        in_specs=[pl.BlockSpec(memory_space=pltpu.VMEM)] * len(arrays),
        out_specs=[pl.BlockSpec(memory_space=pltpu.VMEM)] * len(shapes),
        out_shape=[jax.ShapeDtypeStruct(*shape) for shape in shapes],
        compiler_params=pltpu.CompilerParams(vmem_limit_bytes=16 * MIB),
        cost_estimate=pl.CostEstimate(flops=MIB, bytes_accessed=MIB, transcendentals=0),
        name=name,
    )(*[arrays[k] for k in picked])
    return list(outs)


def far_first(step):
    return sorted(range(3), key=lambda p: ORDERS[p][step] != 1)


def exchange_sums(up, pre):
    widths = [CUTS[p + 1] - CUTS[p] for p in range(3)]
    arrays = [None] * 12
    for n, sums in enumerate((up, pre)):
        for p in far_first(0):
            keep, send = sums[p]
            arrays[p * 4 + n * 2 : p * 4 + n * 2 + 2] = keep, swap(send, ORDERS[p][0])
    pair = [((2, 128, width), dtype) for width in widths for dtype in (F32, BF16)]
    left = joint(first_kernel, "first_sums", arrays, pair, 0)
    for p in far_first(1):
        left[p * 2 + 1] = swap(left[p * 2 + 1], ORDERS[p][1])
    left = joint(second_kernel, "second_sums", left, pair, 1)
    for p in far_first(2):
        left[p * 2 + 1] = swap(left[p * 2 + 1], ORDERS[p][2])
    return joint(third_kernel, "third_sums", left, [((2, 128, width), BF16) for width in widths], 2)


def fourth_kernel(*refs):
    for p in range(3):
        for k in range(2):
            refs[6 + p][k] = refs[p * 2 + k][...]


def gather(parts):
    arrays = [None] * 6
    for p in far_first(1):
        arrays[p * 2 : p * 2 + 2] = parts[p], swap(parts[p], ORDERS[p][1])
    held = joint(fourth_kernel, "fourth_blocks", arrays, [((2, *x.shape), BF16) for x in parts], 1)
    pieces = [None] * 6
    for p in far_first(0):
        pieces[p * 2 : p * 2 + 2] = held[p], swap(held[p], ORDERS[p][0])
    return pieces


def back_part(at, pieces, w, half, total):
    for p, order in enumerate(ORDERS):
        rows = None
        width = CUTS[p + 1] - CUTS[p]
        for h in range(2):
            base = (at[1] if h == 0 else 1 - at[1]) * 2048 + CUTS[p]
            piece = pieces[h * 3 + p][:, 0].reshape(256, width)
            cols = w[:, pl.ds(pl.multiple_of(base, 256), width)]
            part = lax.dot_general(piece, cols, (((1,), (1,)), ((), ())), preferred_element_type=F32)
            rows = part if rows is None else rows + part
        for q, j in enumerate(places(order)[half * 4 : half * 4 + 4]):
            dst = pl.multiple_of(jnp.bitwise_xor(at[0], j) * 64, 64)
            total[pl.ds(dst, 64), :] += rows[q * 64 : (q + 1) * 64]


def held_kernel(at, *refs):
    pieces, w, total = refs[:6], refs[6], refs[7]
    total[...] = jnp.zeros_like(total)
    back_part(at, pieces, w, 0, total)


def came_kernel(at, *refs):
    pieces, w, before, out, total = refs[:6], refs[6], refs[7], refs[8], refs[9]
    total[...] = before[...]
    back_part(at, pieces, w, 1, total)
    low = lower((64, 8, 128))
    c = [total[:, k * 128 : (k + 1) * 128].reshape(64, 8, 128) for k in range(4)]
    r = [pltpu.roll(v, 4, 1) for v in c]
    for t in range(2):
        tile = slice(t * 8, t * 8 + 8)
        out[:, 0, tile] = jnp.where(low, c[2 * t], r[2 * t + 1]).astype(BF16)
        out[:, 1, tile] = jnp.where(low, r[2 * t], c[2 * t + 1]).astype(BF16)


def back_messages(at, pieces, w_in):
    vmem = pl.BlockSpec(memory_space=pltpu.VMEM)
    settings = dict(
        out_specs=vmem,
        compiler_params=pltpu.CompilerParams(vmem_limit_bytes=20 * MIB),
        cost_estimate=pl.CostEstimate(flops=512 * 512 * 4096, bytes_accessed=4 * MIB, transcendentals=0),
    )
    held, came = [[pieces[h * 6 + p * 2 + k] for h in range(2) for p in range(3)] for k in range(2)]
    total = pl.pallas_call(
        held_kernel,
        in_specs=[SCALARS] + [vmem] * 7,
        out_shape=jax.ShapeDtypeStruct((512, 512), F32),
        name="back_held",
        **settings,
    )(at, *held, w_in)
    return pl.pallas_call(
        came_kernel,
        in_specs=[SCALARS] + [vmem] * 8,
        out_shape=pltpu.HBM((64, 2, 16, 128), BF16),
        scratch_shapes=[pltpu.VMEM((512, 512), F32)],
        name="back_messages",
        **settings,
    )(at, *came, w_in, total)


def grads_kernel(at, *refs):
    pieces, (x, cot, grad_in, grad_out), scratch = refs[:12], refs[12:16], refs[16:]
    held, rows, turned, wide_in, wide_out, loads, stores = scratch
    todo = [(p, h) for p in range(3) for h in range(2)]
    arrivals = {}
    for p, h in todo:
        for which in range(2):
            for k in range(2):
                n = h * 6 + p * 2 + k
                target = held.at[which, h * 3 + p, k, :, :, 0 : CUTS[p + 1] - CUTS[p]]
                copy = pltpu.make_async_copy(pieces[n].at[:, which], target, loads.at[which * 12 + n])
                copy.start()
                arrivals[which, h, p, k] = copy
    rows_kernel(x, rows)
    dims = (((0,), (0,)), ((), ()))
    leaving = []

    def send(buffer, target):
        leaving.append(pltpu.make_async_copy(buffer, target, stores.at[len(leaving)]))
        leaving[-1].start()

    for p, h in todo:
        if h == 0:
            for q, j in enumerate(places(ORDERS[p])):
                src = pl.multiple_of(jnp.bitwise_xor(at[0], j) * 64, 64)
                turned[0, q * 64 : (q + 1) * 64, :] = rows[pl.ds(src, 64), :]
                turned[1, q * 64 : (q + 1) * 64, :] = cot[pl.ds(src, 64), :]
        for which in range(2):
            for k in range(2):
                arrivals[which, h, p, k].wait()
            for first in range(0, CUTS[p + 1] - CUTS[p], 256):
                piece = held[which, h * 3 + p, :, :, :, first : first + 256].reshape(512, 256)
                slot = (h * 2048 + CUTS[p] + first) // 256
                base = (at[1] if h == 0 else 1 - at[1]) * 2048 + CUTS[p] + first
                span = pl.ds(pl.multiple_of(base, 256), 256)
                if which == 0:
                    wide_in[slot] = lax.dot_general(turned[0], piece, dims, preferred_element_type=F32)
                    send(wide_in.at[slot], grad_in.at[:, span])
                else:
                    wide_out[slot] = lax.dot_general(piece, turned[1], dims, preferred_element_type=F32)
                    send(wide_out.at[slot], grad_out.at[span, :])
    for copy in leaving:
        copy.wait()


def grads_of(at, pieces, x, cot):
    anywhere, vmem = pl.BlockSpec(memory_space=pl.ANY), pl.BlockSpec(memory_space=pltpu.VMEM)
    pieces = [pltpu.with_memory_space_constraint(p, pltpu.HBM) for p in pieces]
    return pl.pallas_call(
        grads_kernel,
        in_specs=[SCALARS] + [anywhere] * 12 + [vmem] * 2,
        out_specs=[anywhere] * 2,
        out_shape=[pltpu.HBM((512, 4096), F32), pltpu.HBM((4096, 512), F32)],
        scratch_shapes=[
            pltpu.VMEM((2, 6, 2, 2, 128, 768), BF16),
            pltpu.VMEM((512, 512), BF16),
            pltpu.VMEM((2, 512, 512), BF16),
            pltpu.VMEM((16, 512, 256), F32),
            pltpu.VMEM((16, 256, 512), F32),
            pltpu.SemaphoreType.DMA((24,)),
            pltpu.SemaphoreType.DMA((32,)),
        ],
        compiler_params=pltpu.CompilerParams(vmem_limit_bytes=36 * MIB),
        cost_estimate=pl.CostEstimate(flops=4 * 512 * 512 * 4096, bytes_accessed=24 * MIB, transcendentals=0),
        name="grads",
    )(at, *pieces, x, cot)


def act_kernel(x, act, gain, out, twice, back):
    a = act[...].astype(F32)
    twice[0:4, :] = a
    twice[4:8, :] = a
    a = twice[...]
    center = a - jnp.mean(a, axis=1, keepdims=True)
    inverse = lax.rsqrt(jnp.mean(center * center, axis=1, keepdims=True) + EPSILON)
    scaled = center * inverse
    low = lower((8, 128))
    for g in range(16):
        total = x[g // 8 * 64 + g % 8].astype(F32)
        for d in range(1, 8):
            total += x[g // 8 * 64 + d * 8 + g % 8].astype(F32)
        for t in range(2):
            tile = total[t * 8 : t * 8 + 8]
            turned = pltpu.roll(tile, 4, 0)
            at = g * 512 + t * 256
            back[:, at : at + 128] = jnp.where(low, tile, turned)
            back[:, at + 128 : at + 256] = jnp.where(low, turned, tile)
    dxhat = back[...] * gain[...]
    first = jnp.mean(dxhat, axis=1, keepdims=True)
    second = jnp.mean(dxhat * scaled, axis=1, keepdims=True)
    back[...] = inverse * (dxhat - first - scaled * second)
    out[...] = back[0:4, :]


def grad_act_of(x, act, gain):
    return pl.pallas_call(
        act_kernel,
        in_specs=[pl.BlockSpec(memory_space=pltpu.VMEM)] * 3,
        out_specs=pl.BlockSpec(memory_space=pltpu.VMEM),
        out_shape=jax.ShapeDtypeStruct((4, 8192), F32),
        scratch_shapes=[pltpu.VMEM((8, 8192), F32), pltpu.VMEM((8, 8192), F32)],
        compiler_params=pltpu.CompilerParams(vmem_limit_bytes=8 * MIB),
        name="grad_act",
    )(x, act, gain.reshape(1, -1))


def local(act, gain, shift, w_in, w_out, cotangent):
    section, tensor = lax.axis_index("section"), lax.axis_index("tensor")
    core, ring = lax.bitwise_and(tensor, 1), lax.shift_right_logical(tensor, 1)
    bit_a = jnp.where((ring == 1) | (ring == 2), 1, 0)
    number = bit_a * 4 + lax.bitwise_and(ring, 2) + section
    at = jnp.stack([number, core]).astype(jnp.int32)

    out_other = swap(w_out, "core")
    cot_other = swap(cotangent, "core")
    in_other = swap(w_in, "core")
    messages = norm_messages(act, gain, shift)
    mixed = lax.all_to_all(messages.reshape(128, 16, 128), EVERY, 0, 0, tiled=True)
    up = chip_sum(at, cotangent, cot_other, w_out, out_other, True)
    mixed, _ = lax.optimization_barrier((mixed, up[0][0]))
    mixed_other = swap(mixed, "core")
    pre = chip_sum(at, mixed, mixed_other, w_in, in_other, False)
    pieces = gather(exchange_sums(up, pre))
    pieces += [swap(p, "core") for p in pieces]

    share = back_messages(at, pieces, w_in)
    returned = lax.all_to_all(share.reshape(128, 16, 128), EVERY, 0, 0, tiled=True)
    grad_act = grad_act_of(returned, act, gain)
    grad_in, grad_out = grads_of(at, pieces, mixed, cotangent)
    return (grad_in, grad_out, grad_act)


def solution(mesh):
    in_specs = (
        P(EVERY, None),
        P(),
        P(),
        P(OWNERS, "dp"),
        P("dp", OWNERS),
        P(None, OWNERS),
    )
    out_specs = (P(OWNERS, "dp"), P("dp", OWNERS), P(EVERY, None))
    return jax.shard_map(local, mesh=mesh, in_specs=in_specs, out_specs=out_specs, check_vma=False)
```

```python
import functools

import jax
import jax.numpy as jnp
from jax import lax
from jax.experimental import pallas as pl
from jax.experimental.pallas import tpu as pltpu
from jax.sharding import PartitionSpec as P

EPSILON = 1e-05
OWNERS = ("section", "tensor")
EVERY = ("section", "dp", "tensor")
BF16, F32 = jnp.bfloat16, jnp.float32
MIB = 1 << 20

def swap(x, link):
    pairs = []
    for s in range(2):
        for y in range(4):
            for c in range(2):
                if link == "core":
                    s2, y2, c2 = s, y, 1 - c
                else:
                    y2 = y ^ 1 if link & 4 else y
                    y2 = 3 - y2 if link & 2 else y2
                    s2, c2 = s ^ (link & 1), c
                pairs.append((s * 8 + y * 2 + c, s2 * 8 + y2 * 2 + c2))
    return lax.ppermute(x, OWNERS, pairs)


def lower(shape):
    return lax.broadcasted_iota(jnp.int32, shape, len(shape) - 2) % 8 < 4


SCALARS = pl.BlockSpec(memory_space=pltpu.SMEM)


def norm_kernel(act, gain, shift, out, twice):
    x = act[...].astype(F32)
    twice[0:4, :] = x
    twice[4:8, :] = x
    x = twice[...]
    center = x - jnp.mean(x, axis=1, keepdims=True)
    inverse = lax.rsqrt(jnp.mean(center * center, axis=1, keepdims=True) + EPSILON)
    twice[...] = center * inverse * gain[...] + shift[...]
    low = lower((8, 128))
    for g in range(16):
        cols = [twice[:, g * 512 + k * 128 : g * 512 + (k + 1) * 128] for k in range(4)]
        piece = jnp.concatenate([jnp.where(low, cols[0], cols[1]), jnp.where(low, cols[2], cols[3])], axis=0)
        piece = piece.astype(BF16)
        for d in range(8):
            out[g // 8, d, g % 8] = piece


def norm_messages(act, gain, shift):
    return pl.pallas_call(
        norm_kernel,
        out_shape=pltpu.HBM((2, 8, 8, 16, 128), BF16),
        scratch_shapes=[pltpu.VMEM((8, 8192), F32)],
        compiler_params=pltpu.CompilerParams(vmem_limit_bytes=56 * MIB),
        name="norm_messages",
    )(act, gain.reshape(1, -1), shift.reshape(1, -1))


def unfold(even, odd, k, low):
    tile = slice(k // 2 * 8, k // 2 * 8 + 8)
    e, o = even[:, tile], odd[:, tile]
    if k % 2 == 0:
        return jnp.where(low, e, pltpu.roll(o, 4, 1))
    return jnp.where(low, pltpu.roll(e, 4, 1), o)


def rows_kernel(x, out):
    x = x[...].reshape(64, 2, 16, 128)
    even, odd = x[:, 0].astype(F32), x[:, 1].astype(F32)
    low = lower((64, 8, 128))
    for k in range(4):
        out[:, k * 128 : (k + 1) * 128] = unfold(even, odd, k, low).reshape(512, 128).astype(BF16)


ORDERS = ((4, 1, 2), (2, 4, 1), (1, 2, 4))
CUTS = (0, 768, 1536, 2048)


def places(order):
    return [sum(link for k, link in enumerate(order) if q >> (2 - k) & 1) for q in range(8)]


def split(total, first_column, outs):
    last_column = first_column + total.shape[1]
    for p, order in enumerate(ORDERS):
        first, last = max(CUTS[p], first_column), min(CUTS[p + 1], last_column)
        if first >= last:
            continue
        for q, j in enumerate(places(order)):
            out = outs[p * 2 + q // 4]
            block = total[j * 64 : (j + 1) * 64, first - first_column : last - first_column]
            out[q % 4 * 64 : (q % 4 + 1) * 64, first - CUTS[p] : last - CUTS[p]] = block.astype(out.dtype)


def up_kernel(at, x, x_other, w, w_other, *refs):
    outs, (lhs, weights, loads) = refs[:6], refs[6:]
    span = pl.ds(pl.multiple_of(at[1] * 2048, 2048), 2048)
    copies = []
    for n, ref in enumerate((w, w_other)):
        copies.append(pltpu.make_async_copy(ref.at[span, :], weights.at[:, n * 512 : n * 512 + 512], loads.at[n]))
        copies[n].start()
    for j in range(8):
        src = pl.multiple_of(jnp.bitwise_xor(at[0], j) * 64, 64)
        lhs[j * 64 : (j + 1) * 64, 0:512] = x[pl.ds(src, 64), :]
        lhs[j * 64 : (j + 1) * 64, 512:1024] = x_other[pl.ds(src, 64), :]
    for copy in copies:
        copy.wait()
    for first in (0, 1024):
        dims = (((1,), (1,)), ((), ()))
        split(lax.dot_general(lhs[...], weights[first : first + 1024], dims, preferred_element_type=F32), first, outs)


def pre_kernel(at, x, x_other, w, w_other, *refs):
    outs, (lhs, weights, tokens, loads, token_loads) = refs[:6], refs[6:]
    copies = [pltpu.make_async_copy(ref, tokens.at[n], token_loads.at[n]) for n, ref in enumerate((x, x_other))]
    for k in range(2):
        for n, ref in enumerate((w, w_other)):
            source = ref.at[:, pl.ds(pl.multiple_of(at[1] * 2048 + k * 1024, 1024), 1024)]
            target = weights.at[n * 512 : n * 512 + 512, k * 1024 : k * 1024 + 1024]
            copies.append(pltpu.make_async_copy(source, target, loads.at[k * 2 + n]))
    for copy in copies:
        copy.start()
    low = lower((8, 8, 128))
    for n in range(2):
        copies[n].wait()
        for j in range(8):
            some = tokens[n, pl.ds(jnp.bitwise_xor(at[0], j) * 16, 16)].reshape(8, 2, 16, 128)
            even, odd = some[:, 0].astype(F32), some[:, 1].astype(F32)
            for k in range(4):
                rows = unfold(even, odd, k, low).reshape(64, 128).astype(BF16)
                lhs[j * 64 : (j + 1) * 64, n * 512 + k * 128 : n * 512 + (k + 1) * 128] = rows
    for k in range(2):
        copies[2 + 2 * k].wait()
        copies[3 + 2 * k].wait()
        split(jnp.dot(lhs[...], weights[:, k * 1024 : k * 1024 + 1024], preferred_element_type=F32), k * 1024, outs)


HALVES = [
    jax.ShapeDtypeStruct((256, CUTS[p + 1] - CUTS[p]), dtype) for p in range(3) for dtype in (F32, BF16)
]
VMEM_BLOCK, ANY_BLOCK = pl.BlockSpec(memory_space=pltpu.VMEM), pl.BlockSpec(memory_space=pl.ANY)


def in_pairs(arrays):
    return [(arrays[2 * p], arrays[2 * p + 1]) for p in range(3)]


def chip_sum(at, x, x_other, w, w_other, up):
    w, w_other = [pltpu.with_memory_space_constraint(v, pltpu.HBM) for v in (w, w_other)]
    scratch = [pltpu.VMEM((512, 1024), BF16), pltpu.VMEM((2048, 1024) if up else (1024, 2048), BF16)]
    loads = [pltpu.SemaphoreType.DMA((2,))]
    if not up:
        scratch.append(pltpu.VMEM((2, 128, 16, 128), BF16))
        loads.insert(0, pltpu.SemaphoreType.DMA((4,)))
    outs = pl.pallas_call(
        up_kernel if up else pre_kernel,
        in_specs=[SCALARS] + [VMEM_BLOCK if up else ANY_BLOCK] * 2 + [ANY_BLOCK] * 2,
        out_specs=[VMEM_BLOCK] * 6,
        out_shape=HALVES,
        scratch_shapes=scratch + loads,
        compiler_params=pltpu.CompilerParams(vmem_limit_bytes=20 * MIB),
        cost_estimate=pl.CostEstimate(flops=MIB, bytes_accessed=MIB, transcendentals=0),
        name="up_sum" if up else "pre_sum",
    )(at, x, x_other, w, w_other)
    return in_pairs(outs)


def first_kernel(*refs):
    for p in range(3):
        for n in range(2):
            keep, came = refs[p * 4 + n * 2], refs[p * 4 + n * 2 + 1]
            total = keep[...] + came[...].astype(F32)
            refs[12 + p * 2][n] = total[:128]
            refs[13 + p * 2][n] = total[128:].astype(BF16)


def second_kernel(*refs):
    for p in range(3):
        total = refs[p * 2][...] + refs[p * 2 + 1][...].astype(F32)
        refs[6 + p * 2][...] = total
        refs[7 + p * 2][...] = total.astype(BF16)


def third_kernel(*refs):
    for p in range(3):
        keep, came, out = refs[p * 2], refs[p * 2 + 1], refs[6 + p]
        for block in range(2):
            mine, theirs = slice(block * 64, block * 64 + 64), slice(64 - block * 64, 128 - block * 64)
            for first in range(0, out.shape[2], 128):
                cols = slice(first, first + 128)
                up = keep[0, mine, cols] + came[0, theirs, cols].astype(F32)
                v = keep[1, mine, cols] + came[1, theirs, cols].astype(F32)
                square = v * v
                t = jnp.tanh(SLOPE * v * (1.0 + CUBE * square))
                half = 0.5 * (1.0 + t)
                out[1, mine, cols] = (v * half).astype(BF16)
                bend = 0.5 * SLOPE * v * (1.0 - t * t) * (1.0 + 3.0 * CUBE * square)
                out[0, mine, cols] = (up * (half + bend)).astype(BF16)


SLOPE, CUBE = 0.7978845608028654, 0.044715


def joint(kernel, name, arrays, shapes, step):
    each = len(arrays) // 3
    picked = [p * each + k for p in far_first(step) for k in range(each)]

    def body(*refs):
        inputs = [None] * len(picked)
        for place, source in enumerate(picked):
            inputs[source] = refs[place]
        kernel(*inputs, *refs[len(picked) :])

    outs = pl.pallas_call(
        body,
        in_specs=[pl.BlockSpec(memory_space=pltpu.VMEM)] * len(arrays),
        out_specs=[pl.BlockSpec(memory_space=pltpu.VMEM)] * len(shapes),
        out_shape=[jax.ShapeDtypeStruct(*shape) for shape in shapes],
        compiler_params=pltpu.CompilerParams(vmem_limit_bytes=16 * MIB),
        cost_estimate=pl.CostEstimate(flops=MIB, bytes_accessed=MIB, transcendentals=0),
        name=name,
    )(*[arrays[k] for k in picked])
    return list(outs)


def gate_kernel(x, after, out):
    pass


def gate(x, after):
    anywhere = pl.BlockSpec(memory_space=pl.ANY)
    return pl.pallas_call(
        gate_kernel,
        in_specs=[anywhere] * 2,
        out_specs=anywhere,
        out_shape=jax.ShapeDtypeStruct(x.shape, x.dtype),
        input_output_aliases={0: 0},
        cost_estimate=pl.CostEstimate(flops=MIB, bytes_accessed=MIB, transcendentals=0),
        compiler_params=pltpu.CompilerParams(vmem_limit_bytes=MIB),
        name="gate",
    )(x, after)


def far_first(step):
    return sorted(range(3), key=lambda p: ORDERS[p][step] != 1)


def exchange_sums(up, pre):
    widths = [CUTS[p + 1] - CUTS[p] for p in range(3)]
    arrays = [None] * 12
    for n, sums in enumerate((up, pre)):
        for p in far_first(0):
            keep, send = sums[p]
            arrays[p * 4 + n * 2 : p * 4 + n * 2 + 2] = keep, swap(send, ORDERS[p][0])
    pair = [((2, 128, width), dtype) for width in widths for dtype in (F32, BF16)]
    left = joint(first_kernel, "first_sums", arrays, pair, 0)
    for p in far_first(1):
        left[p * 2 + 1] = swap(left[p * 2 + 1], ORDERS[p][1])
    left = joint(second_kernel, "second_sums", left, pair, 1)
    for p in far_first(2):
        left[p * 2 + 1] = swap(left[p * 2 + 1], ORDERS[p][2])
    return joint(third_kernel, "third_sums", left, [((2, 128, width), BF16) for width in widths], 2)


def fourth_kernel(*refs):
    for p in range(3):
        for k in range(2):
            refs[6 + p][k] = refs[p * 2 + k][...]


def gather(parts):
    arrays = [None] * 6
    for p in far_first(1):
        arrays[p * 2 : p * 2 + 2] = parts[p], swap(parts[p], ORDERS[p][1])
    held = joint(fourth_kernel, "fourth_blocks", arrays, [((2, *x.shape), BF16) for x in parts], 1)
    pieces = [None] * 6
    for p in far_first(0):
        pieces[p * 2 : p * 2 + 2] = held[p], swap(held[p], ORDERS[p][0])
    return pieces


def back_part(at, pieces, w, half, total):
    for p, order in enumerate(ORDERS):
        rows = None
        width = CUTS[p + 1] - CUTS[p]
        for h in range(2):
            base = (at[1] if h == 0 else 1 - at[1]) * 2048 + CUTS[p]
            piece = pieces[h * 3 + p][:, 0].reshape(256, width)
            cols = w[:, pl.ds(pl.multiple_of(base, 256), width)]
            part = lax.dot_general(piece, cols, (((1,), (1,)), ((), ())), preferred_element_type=F32)
            rows = part if rows is None else rows + part
        for q, j in enumerate(places(order)[half * 4 : half * 4 + 4]):
            dst = pl.multiple_of(jnp.bitwise_xor(at[0], j) * 64, 64)
            total[pl.ds(dst, 64), :] += rows[q * 64 : (q + 1) * 64]


def held_kernel(at, *refs):
    pieces, w, total = refs[:6], refs[6], refs[7]
    total[...] = jnp.zeros_like(total)
    back_part(at, pieces, w, 0, total)


def came_kernel(at, *refs):
    pieces, w, before, out, total = refs[:6], refs[6], refs[7], refs[8], refs[9]
    total[...] = before[...]
    back_part(at, pieces, w, 1, total)
    low = lower((64, 8, 128))
    c = [total[:, k * 128 : (k + 1) * 128].reshape(64, 8, 128) for k in range(4)]
    r = [pltpu.roll(v, 4, 1) for v in c]
    for t in range(2):
        tile = slice(t * 8, t * 8 + 8)
        out[:, 0, tile] = jnp.where(low, c[2 * t], r[2 * t + 1]).astype(BF16)
        out[:, 1, tile] = jnp.where(low, r[2 * t], c[2 * t + 1]).astype(BF16)


def back_messages(at, pieces, w_in):
    vmem = pl.BlockSpec(memory_space=pltpu.VMEM)
    settings = dict(
        out_specs=vmem,
        compiler_params=pltpu.CompilerParams(vmem_limit_bytes=20 * MIB),
        cost_estimate=pl.CostEstimate(flops=512 * 512 * 4096, bytes_accessed=4 * MIB, transcendentals=0),
    )
    held, came = [[pieces[h * 6 + p * 2 + k] for h in range(2) for p in range(3)] for k in range(2)]
    total = pl.pallas_call(
        held_kernel,
        in_specs=[SCALARS] + [vmem] * 7,
        out_shape=jax.ShapeDtypeStruct((512, 512), F32),
        name="back_held",
        **settings,
    )(at, *held, w_in)
    return pl.pallas_call(
        came_kernel,
        in_specs=[SCALARS] + [vmem] * 8,
        out_shape=pltpu.HBM((64, 2, 16, 128), BF16),
        scratch_shapes=[pltpu.VMEM((512, 512), F32)],
        name="back_messages",
        **settings,
    )(at, *came, w_in, total)


def grads_kernel(at, *refs):
    pieces, (x, cot, grad_in, grad_out), scratch = refs[:12], refs[12:16], refs[16:]
    held, rows, turned, wide_in, wide_out, loads, stores = scratch
    todo = [(p, h) for p in range(3) for h in range(2)]
    arrivals = {}
    for p, h in todo:
        for which in range(2):
            for k in range(2):
                n = h * 6 + p * 2 + k
                target = held.at[which, h * 3 + p, k, :, :, 0 : CUTS[p + 1] - CUTS[p]]
                copy = pltpu.make_async_copy(pieces[n].at[:, which], target, loads.at[which * 12 + n])
                copy.start()
                arrivals[which, h, p, k] = copy
    rows_kernel(x, rows)
    dims = (((0,), (0,)), ((), ()))
    leaving = []

    def send(buffer, target):
        leaving.append(pltpu.make_async_copy(buffer, target, stores.at[len(leaving)]))
        leaving[-1].start()

    for p, h in todo:
        if h == 0:
            for q, j in enumerate(places(ORDERS[p])):
                src = pl.multiple_of(jnp.bitwise_xor(at[0], j) * 64, 64)
                turned[0, q * 64 : (q + 1) * 64, :] = rows[pl.ds(src, 64), :]
                turned[1, q * 64 : (q + 1) * 64, :] = cot[pl.ds(src, 64), :]
        for which in range(2):
            for k in range(2):
                arrivals[which, h, p, k].wait()
            for first in range(0, CUTS[p + 1] - CUTS[p], 256):
                piece = held[which, h * 3 + p, :, :, :, first : first + 256].reshape(512, 256)
                slot = (h * 2048 + CUTS[p] + first) // 256
                base = (at[1] if h == 0 else 1 - at[1]) * 2048 + CUTS[p] + first
                span = pl.ds(pl.multiple_of(base, 256), 256)
                if which == 0:
                    wide_in[slot] = lax.dot_general(turned[0], piece, dims, preferred_element_type=F32)
                    send(wide_in.at[slot], grad_in.at[:, span])
                else:
                    wide_out[slot] = lax.dot_general(piece, turned[1], dims, preferred_element_type=F32)
                    send(wide_out.at[slot], grad_out.at[span, :])
    for copy in leaving:
        copy.wait()


def grads_of(at, pieces, x, cot):
    anywhere, vmem = pl.BlockSpec(memory_space=pl.ANY), pl.BlockSpec(memory_space=pltpu.VMEM)
    pieces = [pltpu.with_memory_space_constraint(p, pltpu.HBM) for p in pieces]
    return pl.pallas_call(
        grads_kernel,
        in_specs=[SCALARS] + [anywhere] * 12 + [vmem] * 2,
        out_specs=[anywhere] * 2,
        out_shape=[pltpu.HBM((512, 4096), F32), pltpu.HBM((4096, 512), F32)],
        scratch_shapes=[
            pltpu.VMEM((2, 6, 2, 2, 128, 768), BF16),
            pltpu.VMEM((512, 512), BF16),
            pltpu.VMEM((2, 512, 512), BF16),
            pltpu.VMEM((16, 512, 256), F32),
            pltpu.VMEM((16, 256, 512), F32),
            pltpu.SemaphoreType.DMA((24,)),
            pltpu.SemaphoreType.DMA((32,)),
        ],
        compiler_params=pltpu.CompilerParams(vmem_limit_bytes=36 * MIB),
        cost_estimate=pl.CostEstimate(flops=4 * 512 * 512 * 4096, bytes_accessed=24 * MIB, transcendentals=0),
        name="grads",
    )(at, *pieces, x, cot)


def act_kernel(x, act, gain, out, twice, back):
    a = act[...].astype(F32)
    twice[0:4, :] = a
    twice[4:8, :] = a
    a = twice[...]
    center = a - jnp.mean(a, axis=1, keepdims=True)
    inverse = lax.rsqrt(jnp.mean(center * center, axis=1, keepdims=True) + EPSILON)
    scaled = center * inverse
    low = lower((8, 128))
    for g in range(16):
        total = x[g // 8 * 64 + g % 8].astype(F32)
        for d in range(1, 8):
            total += x[g // 8 * 64 + d * 8 + g % 8].astype(F32)
        for t in range(2):
            tile = total[t * 8 : t * 8 + 8]
            turned = pltpu.roll(tile, 4, 0)
            at = g * 512 + t * 256
            back[:, at : at + 128] = jnp.where(low, tile, turned)
            back[:, at + 128 : at + 256] = jnp.where(low, turned, tile)
    dxhat = back[...] * gain[...]
    first = jnp.mean(dxhat, axis=1, keepdims=True)
    second = jnp.mean(dxhat * scaled, axis=1, keepdims=True)
    back[...] = inverse * (dxhat - first - scaled * second)
    out[...] = back[0:4, :]


def grad_act_of(x, act, gain):
    return pl.pallas_call(
        act_kernel,
        in_specs=[pl.BlockSpec(memory_space=pltpu.VMEM)] * 3,
        out_specs=pl.BlockSpec(memory_space=pltpu.VMEM),
        out_shape=jax.ShapeDtypeStruct((4, 8192), F32),
        scratch_shapes=[pltpu.VMEM((8, 8192), F32), pltpu.VMEM((8, 8192), F32)],
        compiler_params=pltpu.CompilerParams(vmem_limit_bytes=8 * MIB),
        name="grad_act",
    )(x, act, gain.reshape(1, -1))


def local(act, gain, shift, w_in, w_out, cotangent):
    section, tensor = lax.axis_index("section"), lax.axis_index("tensor")
    core, ring = lax.bitwise_and(tensor, 1), lax.shift_right_logical(tensor, 1)
    bit_a = jnp.where((ring == 1) | (ring == 2), 1, 0)
    number = bit_a * 4 + lax.bitwise_and(ring, 2) + section
    at = jnp.stack([number, core]).astype(jnp.int32)

    out_other = swap(w_out, "core")
    cot_other = swap(cotangent, "core")
    in_other = swap(w_in, "core")
    messages = norm_messages(act, gain, shift)
    mixed = lax.all_to_all(messages.reshape(128, 16, 128), EVERY, 0, 0, tiled=True)
    up = chip_sum(at, cotangent, cot_other, w_out, out_other, True)
    mixed = gate(mixed, up[0][0])
    mixed_other = swap(mixed, "core")
    pre = chip_sum(at, mixed, mixed_other, w_in, in_other, False)
    pieces = gather(exchange_sums(up, pre))
    pieces += [swap(p, "core") for p in pieces]

    share = back_messages(at, pieces, w_in)
    returned = lax.all_to_all(share.reshape(128, 16, 128), EVERY, 0, 0, tiled=True)
    grad_act = grad_act_of(returned, act, gain)
    grad_in, grad_out = grads_of(at, pieces, mixed, cotangent)
    return (grad_in, grad_out, grad_act)


def solution(mesh):
    in_specs = (
        P(EVERY, None),
        P(),
        P(),
        P(OWNERS, "dp"),
        P("dp", OWNERS),
        P(None, OWNERS),
    )
    out_specs = (P(OWNERS, "dp"), P("dp", OWNERS), P(EVERY, None))
    return jax.shard_map(local, mesh=mesh, in_specs=in_specs, out_specs=out_specs, check_vma=False)
```
